128 devices in a mesh: blk: 32 (over y_hi, z, x), grp: 4 (over y_lo, core).
Axes of the slice: x: 4, y: 4 (y_hi: 2, y_lo: 2; y = y_hi * 2 + y_lo), z: 4, core: 2. Of those that a mesh axis runs over, the one named last changes fastest.
Arguments:
- coulomb_factors: bfloat16 [49152, 4096], P('blk', 'grp'), may hold values from -0.0546875 to 0.0546875
- energy_gaps: float32 [49152], P('blk'), may hold values from 0.2 to 5
- frequencies: float32 [2], replicated, may hold values from 0.3 to 2.5
Outputs:
- polar: float32 [4096, 2, 4096], P('blk', None, 'grp')
The draws below stay inside these ranges and needn't reach their ends.
All inputs are finite; a program needn't handle non-finite values.
Results may differ from the reference program's by a relative error of at most 0.00085.
Values may be sent and summed in bfloat16 or wider, within the bound.
No kernel may reach another device: no remote copies, remote signals or barrier semaphores. Data moves between devices by JAX's collectives and lax.ppermute only.
A program may use at most 128 MiB of HBM per device.

```python
import math
import jax
import jax.numpy as jnp
from jax import lax

NAUX = 4096
FREQ = 2
ROWS = 49152


def spiked(array, rng, source, target, shards_of, factor):
    def block_of(position):
        return (jnp.arange(array.shape[position]) // (array.shape[position] // shards_of)).reshape((-1,) + (1,) * (array.ndim - 1 - position))

    first = jax.random.permutation(rng, shards_of)[block_of(target)]
    far = (block_of(target) + shards_of // 2) % shards_of
    return jnp.where((block_of(source) == first) | (block_of(source) == far), factor * array, array)


def level_of(own_key, shape, cuts, least, high):
    level = 1.0
    for axis_at, blocks in cuts:
        steps = jax.random.uniform(jax.random.fold_in(jax.random.fold_in(own_key, 6), axis_at), (blocks,), jnp.float32, least / len(cuts), high / len(cuts))
        level = level * jnp.repeat(jnp.exp(steps), shape[axis_at] // blocks).reshape((-1,) + (1,) * (len(shape) - 1 - axis_at))
    return level


def bell_draw_with(key, dims, width, bound, cuts, heavy, kind=jnp.bfloat16):
    drawn = width * jax.random.normal(key, dims, jnp.float32)
    if cuts:
        drawn = drawn * level_of(key, dims, cuts, -0.22, 0.18)
    return jnp.clip(spiked(drawn, jax.random.fold_in(key, 3), *heavy), -bound, bound).astype(kind)


def setup_inputs(seed: int = 0) -> dict:
    key_of = jax.random.split(jax.random.key(seed), 4)
    return {
        "coulomb_factors": bell_draw_with(key_of[0], (ROWS, NAUX), ROWS ** -0.5, 0.0546875, ((0, 32), (1, 4)), (0, 1, 32, 2.75)),
        "energy_gaps": jnp.clip(jnp.exp(math.log(5.0) - 3.218876 * jax.random.uniform(key_of[1], (ROWS,), jnp.float32) ** level_of(key_of[1], (ROWS,), ((0, 32),), -0.2, 0.2)), 0.2, 5.0),
        "frequencies": jnp.clip(jax.random.uniform(key_of[2], (FREQ,), jnp.float32, 0.3, 2.5), 0.3, 2.5),
    }


def reference(coulomb_factors, energy_gaps, frequencies):
    weights = 4.0 * energy_gaps[:, None] / (energy_gaps[:, None] ** 2 + frequencies[None, :] ** 2)
    scaled = (coulomb_factors[:, None, :].astype(jnp.float32) * weights[:, :, None]).astype(jnp.bfloat16)
    flat = scaled.reshape(scaled.shape[0], FREQ * NAUX)
    total = lax.dot_general(coulomb_factors, flat, (((0,), (0,)), ((), ())), preferred_element_type=jnp.float32)
    return total.reshape(NAUX, FREQ, NAUX)
```

```python
import functools

import jax
import jax.numpy as jnp
import numpy as np
from jax import lax
from jax.experimental import pallas as pl
from jax.experimental.pallas import tpu as pltpu
from jax.sharding import PartitionSpec as P

AXES = ("blk", "grp")
FREQ = 2
T = 128
FAR = (2, 3, 1, 0)
VMEM = 56 * 1024 * 1024


def parts_of(d):
    x, z, y_hi, grp = (d >> 2) & 3, (d >> 4) & 3, d >> 6, d & 3
    return (y_hi, x, z, grp) if grp & 1 == 0 else (y_hi, z, x, grp)


def device(y_hi, s1, s2, grp):
    x, z = (s1, s2) if grp & 1 == 0 else (s2, s1)
    return (((y_hi * 4 + z) * 4 + x) << 2) + grp


def shift_perm(d1=0, d2=0, dy=0):
    pairs = []
    for d in range(128):
        y_hi, s1, s2, grp = parts_of(d)
        pairs.append((d, device(y_hi ^ dy, (s1 + d1) & 3, (s2 + d2) & 3, grp)))
    return pairs


def group_perm(source):
    return [(blk * 4 + source(grp), blk * 4 + grp) for blk in range(32) for grp in range(4)]


def messages(d):
    y_hi, s1, s2, g = parts_of(d)
    far, mate, core = FAR[g], g ^ 1, g & 1
    own = lambda half: 8 * g + 4 * half
    return [
        ((8 * far + s1) * 4 + g, y_hi * 4 + s2),
        ((8 * far + 4 + s1) * 4 + g, y_hi * 4 + s2),
        ((own(0) + s2) * 4 + far, y_hi * 4 + s1),
        ((own(1) + s2) * 4 + far, y_hi * 4 + s1),
        ((own(0) + s1) * 4 + g, y_hi * 4 + s2),
        ((own(1) + s2) * 4 + g, y_hi * 4 + s1),
        ((8 * mate + 4 * y_hi + s1) * 4 + g, core * 4 + s2),
        ((own(y_hi) + s2) * 4 + mate, core * 4 + s1),
    ]


@functools.cache
def rounds():
    left = [messages(d) for d in range(128)]
    todo = [set(range(8)) for _ in range(128)]
    perms, sent, filled = [], np.zeros((8, 128), np.int32), np.zeros((8, 128), np.int32)
    for k in range(8):
        taken = {}

        def place(d, seen):
            for m in sorted(todo[d]):
                to = left[d][m][0]
                if to in seen:
                    continue
                seen.add(to)
                if to not in taken or place(taken[to][0], seen):
                    taken[to] = (d, m)
                    return True
            return False

        for d in range(128):
            place(d, set())
        perms.append([(d, to) for to, (d, _) in sorted(taken.items())])
        for to, (d, m) in taken.items():
            todo[d].remove(m)
            sent[k, d] = m
            filled[k, to] = left[d][m][1]
    return perms, sent, filled


def permute(value, pairs):
    return lax.ppermute(value, AXES, pairs)


def params():
    return pltpu.CompilerParams(vmem_limit_bytes=VMEM)


def product(lhs, rhs):
    return lax.dot_general(lhs, rhs, (((0,), (0,)), ((), ())), preferred_element_type=jnp.float32)


def scatter_blocks(place, total, outs, n):
    for d in range(4):
        rows = pl.ds(pl.multiple_of(((place[0] + d) & 3) * T, T), T)
        for e in range(4):
            columns = pl.ds(pl.multiple_of(((place[1] + e) & 3) * T, T), T)
            outs[d][e, n] = total[rows, columns].astype(outs[d].dtype)


def block_shapes(count):
    return [jax.ShapeDtypeStruct((4, count, T, T), jnp.float32 if d == 0 else jnp.bfloat16) for d in range(4)]


def own_kernel(place, own, weights, scaled, *rest):
    outs, total = rest[:4], rest[4]
    t = pl.program_id(0)
    h, f = t // 2, t % 2
    weight = jnp.where(f == 0, weights[:, 0:1], weights[:, 1:2])
    columns = pl.ds(pl.multiple_of(h * 512, 512), 512)
    scaled[...] = (own[:, columns].astype(jnp.float32) * weight).astype(jnp.bfloat16)
    total[...] = product(own[:, :512], scaled[...])
    scatter_blocks(place, total, outs, f * 3 + h)

    @pl.when(h == 1)
    def _():
        total[...] = product(own[:, 512:], scaled[...])
        scatter_blocks(place, total, outs, f * 3 + 2)


def own_products(place, own, weights):
    rows = own.shape[0]
    whole = lambda *shape: pl.BlockSpec(shape, lambda t, place: (0,) * len(shape))
    return pl.pallas_call(
        own_kernel,
        out_shape=[jax.ShapeDtypeStruct((rows, 2048), jnp.bfloat16)] + block_shapes(6),
        grid_spec=pltpu.PrefetchScalarGridSpec(
            num_scalar_prefetch=1,
            grid=(4,),
            in_specs=[whole(rows, 1024), whole(rows, FREQ)],
            out_specs=[pl.BlockSpec((rows, 512), lambda t, place: (0, (t % 2) * 2 + t // 2))] + [whole(4, 6, T, T)] * 4,
            scratch_shapes=[pltpu.VMEM((512, 512), jnp.float32)],
        ),
        compiler_params=params(),
        cost_estimate=pl.CostEstimate(flops=2 * 6 * 512 * 512 * rows, bytes_accessed=14 * 2**20, transcendentals=0),
        name="own_products",
    )(place, own, weights)


def cross_kernel(place, other, scaled, *rest):
    outs, total = rest[:4], rest[4]
    total[...] = product(other[...], scaled[...])
    scatter_blocks(place, total, outs, 0)


def cross_products(place, other, scaled, mate):
    rows = other.shape[0]
    if mate:
        left = lambda t, place: (0, t // 2)
        right = lambda t, place: (0, place[3] * 2 + t % 2)
    else:
        left = lambda t, place: (0, 0)
        right = lambda t, place: (0, t)
    return pl.pallas_call(
        cross_kernel,
        out_shape=block_shapes(4),
        grid_spec=pltpu.PrefetchScalarGridSpec(
            num_scalar_prefetch=1,
            grid=(4,),
            in_specs=[pl.BlockSpec((rows, 512), left), pl.BlockSpec((rows, 512), right)],
            out_specs=[pl.BlockSpec((4, 1, T, T), lambda t, place: (0, t, 0, 0))] * 4,
            scratch_shapes=[pltpu.VMEM((512, 512), jnp.float32)],
        ),
        compiler_params=params(),
        cost_estimate=pl.CostEstimate(flops=2 * 4 * 512 * 512 * rows, bytes_accessed=12 * 2**20, transcendentals=0),
        name="cross_products",
    )(place, other, scaled)


def first_sum_kernel(kept, a, b, c, *outs):
    for e in range(4):
        outs[e][...] = kept[e] + (a[e].astype(jnp.float32) + b[e].astype(jnp.float32)) + c[e].astype(jnp.float32)


def first_sum(kept, a, b, c):
    count = kept.shape[1]
    wide = pl.BlockSpec((4, 1, T, T), lambda t: (0, t, 0, 0))
    return pl.pallas_call(
        first_sum_kernel,
        out_shape=[jax.ShapeDtypeStruct((count, T, T), jnp.float32)] * 4,
        grid=(count,),
        in_specs=[wide] * 4,
        out_specs=[pl.BlockSpec((1, T, T), lambda t: (t, 0, 0))] * 4,
        compiler_params=params(),
        cost_estimate=pl.CostEstimate(flops=12 * count * T * T, bytes_accessed=56 * count * T * T, transcendentals=0),
        name="first_sum",
    )(kept, a, b, c)


def second_sum_kernel(place, kept, a, b, c, keep, send, total):
    total[...] = (kept[...] + a[...]) + (b[...] + c[...])
    half = total.shape[0] // 2
    for n in range(half):
        keep[n] = total[place[2] * half + n]
        send[n] = total[(1 - place[2]) * half + n]


def second_sum(place, kept, a, b, c):
    count = kept.shape[0]
    vmem = pl.BlockSpec(memory_space=pltpu.VMEM)
    return pl.pallas_call(
        second_sum_kernel,
        out_shape=[jax.ShapeDtypeStruct((count // 2, T, T), jnp.float32)] * 2,
        in_specs=[pl.BlockSpec(memory_space=pltpu.SMEM)] + [vmem] * 4,
        out_specs=[vmem] * 2,
        scratch_shapes=[pltpu.VMEM((count, T, T), jnp.float32)],
        compiler_params=params(),
        cost_estimate=pl.CostEstimate(flops=3 * count * T * T, bytes_accessed=20 * count * T * T, transcendentals=0),
        name="second_sum",
    )(place, kept, a, b, c)


def pack_kernel(place, order, far0, far0_in, far1, far1_in, tri, tri_in, mate, mate_in, *rest):
    outs, ready, total = rest[:8], rest[8], rest[9]
    y_hi = place[2]
    far = [[far0[h] + far0_in[h] for h in range(2)], [far1[h] + far1_in[h] for h in range(2)]]
    for half in range(2):
        for h in range(2):
            ready[half, h] = far[half][h]
            ready[2 + h, half] = far[half][h].T
    own = [tri[j] + tri_in[j] for j in range(3)]
    ready[4, 0] = own[0]
    ready[4, 1] = own[1]
    ready[5, 0] = own[1].T
    ready[5, 1] = own[2].T
    total[...] = mate[...] + mate_in[...]
    for h in range(2):
        ready[6, h] = total[2 * y_hi + h]
        ready[7, h] = total[2 * h + y_hi].T
    for k in range(8):
        outs[k][...] = ready[order[k]]


def pack(place, order, *arrays):
    vmem, smem = pl.BlockSpec(memory_space=pltpu.VMEM), pl.BlockSpec(memory_space=pltpu.SMEM)
    return pl.pallas_call(
        pack_kernel,
        out_shape=[jax.ShapeDtypeStruct((2, T, T), jnp.float32)] * 8,
        in_specs=[smem] * 2 + [vmem] * 8,
        out_specs=[vmem] * 8,
        scratch_shapes=[pltpu.VMEM((8, 2, T, T), jnp.float32), pltpu.VMEM((4, T, T), jnp.float32)],
        compiler_params=params(),
        cost_estimate=pl.CostEstimate(flops=2 * 2**20, bytes_accessed=3 * 2**20, transcendentals=0),
        name="pack",
    )(place, order, *arrays)


def unpack_kernel(slot, *rest):
    arrived, out, ready = rest[:8], rest[8], rest[9]
    for k in range(8):
        ready[slot[k]] = arrived[k][...]
    for f in range(FREQ):
        for i in range(4):
            for h in range(2):
                out[:, f, (4 * h + i) * T : (4 * h + i + 1) * T] = ready[f * 4 + i, h]


def unpack(slot, arrived):
    vmem, smem = pl.BlockSpec(memory_space=pltpu.VMEM), pl.BlockSpec(memory_space=pltpu.SMEM)
    return pl.pallas_call(
        unpack_kernel,
        out_shape=jax.ShapeDtypeStruct((T, FREQ, 1024), jnp.float32),
        in_specs=[smem] + [vmem] * 8,
        out_specs=vmem,
        scratch_shapes=[pltpu.VMEM((8, 2, T, T), jnp.float32)],
        compiler_params=params(),
        cost_estimate=pl.CostEstimate(flops=2**20, bytes_accessed=2 * 2**20, transcendentals=0),
        name="unpack",
    )(slot, *arrived)


def reduced(kept, *send):
    first = first_sum(kept, *(permute(v, shift_perm(d1=d + 1)) for d, v in enumerate(send)))
    return first[0], *(permute(v, shift_perm(d2=e + 1)) for e, v in enumerate(first[1:]))


def on_device(own, energy_gaps, frequencies):
    blk, grp = lax.axis_index("blk"), lax.axis_index("grp")
    x, z, y_hi, core = blk & 3, (blk >> 2) & 3, blk >> 4, grp & 1
    place = jnp.stack([jnp.where(core == 0, x, z), jnp.where(core == 0, z, x), y_hi, core]).astype(jnp.int32)
    perms, sent, filled = rounds()
    me = blk * 4 + grp
    order = lax.dynamic_index_in_dim(jnp.asarray(sent.T), me, 0, keepdims=False)
    slot = lax.dynamic_index_in_dim(jnp.asarray(filled.T), me, 0, keepdims=False)

    weights = 4.0 * energy_gaps[:, None] / (energy_gaps[:, None] ** 2 + frequencies[None, :] ** 2)
    mate = permute(own, group_perm(lambda g: g ^ 1))
    far = [permute(own[:, 512 * h : 512 * (h + 1)], group_perm(lambda g: FAR[g])) for h in range(2)]
    scaled, *tri = own_products(place, own, weights)
    tri = reduced(*tri)
    side = reduced(*cross_products(place, mate, scaled, True))
    cross = [reduced(*cross_products(place, far[h], scaled, False)) for h in range(2)]

    swap = shift_perm(dy=1)
    inputs = []
    for part in cross + [tri]:
        keep, send = second_sum(place, *part)
        inputs += [keep, permute(send, swap)]
    total = (side[0] + side[1]) + (side[2] + side[3])
    inputs += [total, permute(total, swap)]
    packed = pack(place, order, *inputs)
    return unpack(slot, [permute(v, p) for v, p in zip(packed, perms)])


def solution(mesh):
    in_specs = (P("blk", "grp"), P("blk"), P())
    out_specs = P("blk", None, "grp")
    return jax.shard_map(
        on_device, mesh=mesh, in_specs=in_specs, out_specs=out_specs, check_vma=False
    )
```

```python
import functools

import jax
import jax.numpy as jnp
import numpy as np
from jax import lax
from jax.experimental import pallas as pl
from jax.experimental.pallas import tpu as pltpu
from jax.sharding import PartitionSpec as P

AXES = ("blk", "grp")
FREQ = 2
T = 128
FAR = (2, 3, 1, 0)
VMEM = 24 * 1024 * 1024


def parts_of(d):
    x, z, y_hi, grp = (d >> 2) & 3, (d >> 4) & 3, d >> 6, d & 3
    return (y_hi, x, z, grp) if grp & 1 == 0 else (y_hi, z, x, grp)


def device(y_hi, s1, s2, grp):
    x, z = (s1, s2) if grp & 1 == 0 else (s2, s1)
    return (((y_hi * 4 + z) * 4 + x) << 2) + grp


def shift_perm(d1=0, d2=0, dy=0):
    pairs = []
    for d in range(128):
        y_hi, s1, s2, grp = parts_of(d)
        pairs.append((d, device(y_hi ^ dy, (s1 + d1) & 3, (s2 + d2) & 3, grp)))
    return pairs


def group_perm(source):
    return [(blk * 4 + source(grp), blk * 4 + grp) for blk in range(32) for grp in range(4)]


def block_of(core, s1, s2):
    skew = (s1 + s2) & 3
    return (s1, skew) if core == 0 else (skew, s2)


def messages(d):
    y_hi, s1, s2, g = parts_of(d)
    s1, s2 = block_of(g & 1, s1, s2)
    row = lambda group, half, block, grp: (8 * group + 4 * half + block) * 4 + grp
    if y_hi == g >> 1:
        return [
            (row(g, 0, s1, g), s2),
            (row(g, 1, s2, g), s1),
            (row(g, 0, s2, g ^ 1), s1),
            (row(g, 1, s2, g ^ 1), s1),
        ]
    far = FAR[g]
    return [
        (row(far, 0, s1, g), s2),
        (row(far, 1, s1, g), s2),
        (row(g, 0, s2, far), s1),
        (row(g, 1, s2, far), s1),
    ]


@functools.cache
def rounds():
    left = [messages(d) for d in range(128)]
    todo = [set(range(4)) for _ in range(128)]
    perms, sent, filled = [], np.zeros((4, 128), np.int32), np.zeros((4, 128), np.int32)
    for k in range(4):
        taken = {}

        def place(d, seen):
            for m in sorted(todo[d]):
                to = left[d][m][0]
                if to in seen:
                    continue
                seen.add(to)
                if to not in taken or place(taken[to][0], seen):
                    taken[to] = (d, m)
                    return True
            return False

        for d in range(128):
            place(d, set())
        perms.append([(d, to) for to, (d, _) in sorted(taken.items())])
        for to, (d, m) in taken.items():
            todo[d].remove(m)
            sent[k, d] = m
            filled[k, to] = left[d][m][1]
    return perms, sent, filled


def permute(value, pairs):
    return lax.ppermute(value, AXES, pairs)


def call(kernel, out_shape, scalars, arrays, scratch=(), flops=0, name=None):
    vmem, smem = pl.BlockSpec(memory_space=pltpu.VMEM), pl.BlockSpec(memory_space=pltpu.SMEM)
    size = 0
    return pl.pallas_call(
        kernel,
        out_shape=out_shape,
        in_specs=[smem] * len(scalars) + [vmem] * len(arrays),
        out_specs=[vmem] * len(out_shape),
        scratch_shapes=list(scratch),
        compiler_params=pltpu.CompilerParams(vmem_limit_bytes=VMEM),
        cost_estimate=pl.CostEstimate(flops=flops, bytes_accessed=size, transcendentals=0),
        name=name,
    )(*scalars, *arrays)


def floats(*shape):
    return jax.ShapeDtypeStruct(shape, jnp.float32)


def product(lhs, rhs):
    return lax.dot_general(lhs, rhs, (((0,), (0,)), ((), ())), preferred_element_type=jnp.float32)


def scatter_blocks(place, total, outs, n):
    for d in range(4):
        for e in range(4):
            s1, s2 = (place[0] + d) & 3, (place[1] + e) & 3
            skew = (s1 + s2) & 3
            rows = pl.ds(pl.multiple_of(jnp.where(place[3] == 0, s1, skew) * T, T), T)
            columns = pl.ds(pl.multiple_of(jnp.where(place[3] == 0, skew, s2) * T, T), T)
            outs[d][e, n] = total[rows, columns].astype(outs[d].dtype)


def block_shapes(count):
    return [jax.ShapeDtypeStruct((4, count, T, T), jnp.float32 if d == 0 else jnp.bfloat16) for d in range(4)]


def own_kernel(place, own, weights, scaled, *rest):
    outs, total = rest[:4], rest[4]

    def step(t, _):
        h, f = t // 2, t % 2
        weight = jnp.where(f == 0, weights[:, 0:1], weights[:, 1:2])
        columns = pl.ds(pl.multiple_of(h * 512, 512), 512)
        part = 2 * f + h
        scaled[part] = (own[:, columns].astype(jnp.float32) * weight).astype(jnp.bfloat16)
        total[...] = product(own[:, :512], scaled[part])
        scatter_blocks(place, total, outs, f * 3 + h)

        @pl.when(h == 1)
        def _():
            total[...] = product(own[:, 512:], scaled[part])
            scatter_blocks(place, total, outs, f * 3 + 2)

        return 0

    lax.fori_loop(0, 4, step, 0)


def own_products(place, own, weights):
    rows = own.shape[0]
    return call(
        own_kernel,
        [jax.ShapeDtypeStruct((4, rows, 512), jnp.bfloat16)] + block_shapes(6),
        [place],
        [own, weights],
        [pltpu.VMEM((512, 512), jnp.float32)],
        flops=2 * 6 * 512 * 512 * rows,
        name="own_products",
    )


def mate_kernel(place, other, scaled, *rest):
    outs, total = rest[:4], rest[4]

    def step(t, _):
        columns = pl.ds(pl.multiple_of(t // 2 * 512, 512), 512)
        total[...] = product(other[:, columns], scaled[2 * place[3] + t % 2])
        scatter_blocks(place, total, outs, t)
        return 0

    lax.fori_loop(0, 4, step, 0)


def far_kernel(place, other, scaled, *rest):
    outs, total = rest[:4], rest[4]

    def step(t, _):
        total[...] = product(other[...], scaled[t])
        scatter_blocks(place, total, outs, t)
        return 0

    lax.fori_loop(0, 4, step, 0)


def cross_products(kernel, place, other, scaled, name):
    return call(
        kernel,
        block_shapes(4),
        [place],
        [other, scaled],
        [pltpu.VMEM((512, 512), jnp.float32)],
        flops=2 * 4 * 512 * 512 * other.shape[0],
        name=name,
    )


def first_sum_kernel(kept, a, b, c, *outs):
    for e in range(4):
        outs[e][...] = kept[e] + (a[e].astype(jnp.float32) + b[e].astype(jnp.float32)) + c[e].astype(jnp.float32)


def first_sum(kept, a, b, c):
    count = kept.shape[1]
    return call(first_sum_kernel, [floats(count, T, T)] * 4, [], [kept, a, b, c], flops=12 * count * T * T, name="first_sum")


def pack_kernel(place, order, near, twin, far0, far0_in, far1, far1_in, *rest):
    outs, ready = rest[:4], rest[4]
    at_home = place[4] == 1

    @pl.when(at_home)
    def _():
        core = place[3]
        for f in range(FREQ):
            low, both, high = (near[3 * f + j] for j in range(3))
            ready[0, f, 0] = low
            ready[0, f, 1] = both
            ready[1, f, 0] = both.T
            ready[1, f, 1] = high.T
        for k in range(2):
            for h in range(2):
                ready[2 + k, core, h] = near[6 + 2 * h + k].T
                ready[2 + k, 1 - core, h] = twin[2 * k + h]

    @pl.when(jnp.logical_not(at_home))
    def _():
        for half, (part, arrived) in enumerate(((far0, far0_in), (far1, far1_in))):
            for f in range(FREQ):
                for h in range(2):
                    value = part[2 * f + h] + arrived[2 * f + h]
                    ready[half, f, h] = value
                    ready[2 + h, f, half] = value.T

    for k in range(4):
        outs[k][...] = ready[order[k]]


def pack(place, order, *arrays):
    return call(
        pack_kernel,
        [floats(FREQ, 2, T, T)] * 4,
        [place, order],
        arrays,
        [pltpu.VMEM((4, FREQ, 2, T, T), jnp.float32)],
        flops=2**20,
        name="pack",
    )


def unpack_kernel(slot, a, b, c, d, out):
    for k, arrived in enumerate((a, b, c, d)):
        for f in range(FREQ):
            for h in range(2):
                out[:, f, pl.ds(pl.multiple_of(512 * h + slot[k] * T, T), T)] = arrived[f, h]


def unpack(slot, arrived):
    return call(unpack_kernel, [floats(T, FREQ, 1024)], [slot], arrived, flops=2**18, name="unpack")[0]


def after(value, earlier):
    return value if earlier is None else lax.optimization_barrier((value, earlier))[0]


def send_first(send, earlier):
    return [permute(after(v, w), shift_perm(d1=d + 1)) for d, (v, w) in enumerate(zip(send, earlier))]


def send_second(send, earlier):
    return [permute(after(v, w), shift_perm(d2=e + 1)) for e, (v, w) in enumerate(zip(send, earlier))]


def across(value, at_home):
    pairs = [(s, d) for s, d in shift_perm(dy=1) if ((d >> 6) == (d & 3) >> 1) == at_home]
    return permute(value, pairs)


def on_device(own, energy_gaps, frequencies):
    blk, grp = lax.axis_index("blk"), lax.axis_index("grp")
    x, z, y_hi, core = blk & 3, (blk >> 2) & 3, blk >> 4, grp & 1
    home = jnp.where(y_hi == grp >> 1, 1, 0)
    place = jnp.stack([jnp.where(core == 0, x, z), jnp.where(core == 0, z, x), y_hi, core, home]).astype(jnp.int32)
    perms, sent, filled = rounds()
    me = blk * 4 + grp
    order = lax.dynamic_index_in_dim(jnp.asarray(sent.T), me, 0, keepdims=False)
    slot = lax.dynamic_index_in_dim(jnp.asarray(filled.T), me, 0, keepdims=False)

    weights = 4.0 * energy_gaps[:, None] / (energy_gaps[:, None] ** 2 + frequencies[None, :] ** 2)
    swap = group_perm(lambda g: g ^ 1)
    halves = [own[:, :512], own[:, 512:]]
    own, *halves = lax.optimization_barrier((own, *halves))
    far_perm = group_perm(lambda g: FAR[g])
    other = permute(own, swap)
    far0 = permute(halves[0], far_perm)
    far1 = permute(after(halves[1], far0), far_perm)

    scaled, tri, *send = own_products(place, own, weights)
    tri_sent = send_first(send, [None] * 3)
    mate, *send = cross_products(mate_kernel, place, other, scaled, "mate_products")
    mate_sent = send_first(send, tri_sent)
    tri, *tri_send = first_sum(tri, *tri_sent)
    mate, *mate_send = first_sum(mate, *mate_sent)
    sums = [jnp.concatenate(v) for v in zip([tri, *tri_send], [mate, *mate_send])]
    near, near_send = sums[0], sums[1:]

    far0, *send = cross_products(far_kernel, place, far0, scaled, "far_products")
    far0_sent = send_first(send, mate_sent)
    near_sent = send_second(near_send, far0_sent)
    far0, *send = first_sum(far0, *far0_sent)
    far0_sent = send_second(send, near_sent)
    far1, *send = cross_products(far_kernel, place, far1, scaled, "far_products")
    far1_sent = send_first(send, far0_sent)
    far1, *send = first_sum(far1, *far1_sent)
    far1_sent = send_second(send, [None] * 3)

    near = near + near_sent[0] + near_sent[1] + near_sent[2]
    near = near + across(near, True)
    far0 = far0 + far0_sent[0] + far0_sent[1] + far0_sent[2]
    far1 = far1 + far1_sent[0] + far1_sent[1] + far1_sent[2]
    twin = permute(near[6:], swap)
    inputs = [near, twin, far0, across(far0, False), far1, across(far1, False)]
    packed = pack(place, order, *inputs)
    return unpack(slot, [permute(v, p) for v, p in zip(packed, perms)])


def solution(mesh):
    in_specs = (P("blk", "grp"), P("blk"), P())
    out_specs = P("blk", None, "grp")
    return jax.shard_map(
        on_device, mesh=mesh, in_specs=in_specs, out_specs=out_specs, check_vma=False
    )
```

```python
import functools

import jax
import jax.numpy as jnp
import numpy as np
from jax import lax
from jax.experimental import pallas as pl
from jax.experimental.pallas import tpu as pltpu
from jax.sharding import PartitionSpec as P

AXES = ("blk", "grp")
FREQ = 2
T = 128
FAR = (2, 3, 1, 0)
VMEM = 8 * 1024 * 1024


def parts_of(d):
    x, z, y_hi, grp = (d >> 2) & 3, (d >> 4) & 3, d >> 6, d & 3
    return (y_hi, x, z, grp) if grp & 1 == 0 else (y_hi, z, x, grp)


def device(y_hi, s1, s2, grp):
    x, z = (s1, s2) if grp & 1 == 0 else (s2, s1)
    return (((y_hi * 4 + z) * 4 + x) << 2) + grp


def shift_perm(d1=0, d2=0, dy=0):
    pairs = []
    for d in range(128):
        y_hi, s1, s2, grp = parts_of(d)
        pairs.append((d, device(y_hi ^ dy, (s1 + d1) & 3, (s2 + d2) & 3, grp)))
    return pairs


def group_perm(source):
    return [(blk * 4 + source(grp), blk * 4 + grp) for blk in range(32) for grp in range(4)]


def block_of(core, s1, s2):
    skew = (s1 + s2) & 3
    return (s1, skew) if core == 0 else (skew, s2)


def messages(d):
    y_hi, s1, s2, g = parts_of(d)
    s1, s2 = block_of(g & 1, s1, s2)
    row = lambda group, half, block, grp: (8 * group + 4 * half + block) * 4 + grp
    if y_hi == g >> 1:
        return [
            (row(g, 0, s1, g), s2),
            (row(g, 1, s2, g), s1),
            (row(g, 0, s2, g ^ 1), s1),
            (row(g, 1, s2, g ^ 1), s1),
        ]
    far = FAR[g]
    return [
        (row(far, 0, s1, g), s2),
        (row(far, 1, s1, g), s2),
        (row(g, 0, s2, far), s1),
        (row(g, 1, s2, far), s1),
    ]


@functools.cache
def rounds():
    left = [messages(d) for d in range(128)]
    todo = [set(range(4)) for _ in range(128)]
    perms, sent, filled = [], np.zeros((4, 128), np.int32), np.zeros((4, 128), np.int32)
    for k in range(4):
        taken = {}

        def place(d, seen):
            for m in sorted(todo[d]):
                to = left[d][m][0]
                if to in seen:
                    continue
                seen.add(to)
                if to not in taken or place(taken[to][0], seen):
                    taken[to] = (d, m)
                    return True
            return False

        for d in range(128):
            place(d, set())
        perms.append([(d, to) for to, (d, _) in sorted(taken.items())])
        for to, (d, m) in taken.items():
            todo[d].remove(m)
            sent[k, d] = m
            filled[k, to] = left[d][m][1]
    return perms, sent, filled


def permute(value, pairs):
    return lax.ppermute(value, AXES, pairs)


def call(kernel, out_shape, scalars, arrays, scratch=(), flops=0, name=None, aliases=()):
    vmem, smem = pl.BlockSpec(memory_space=pltpu.VMEM), pl.BlockSpec(memory_space=pltpu.SMEM)
    size = 0
    return pl.pallas_call(
        kernel,
        out_shape=out_shape,
        in_specs=[smem] * len(scalars) + [vmem] * len(arrays),
        out_specs=[vmem] * len(out_shape),
        scratch_shapes=list(scratch),
        input_output_aliases=dict(aliases),
        compiler_params=pltpu.CompilerParams(vmem_limit_bytes=VMEM),
        cost_estimate=pl.CostEstimate(flops=flops, bytes_accessed=size, transcendentals=0),
        name=name,
    )(*scalars, *arrays)


def floats(*shape):
    return jax.ShapeDtypeStruct(shape, jnp.float32)


def product(lhs, rhs):
    return lax.dot_general(lhs, rhs, (((0,), (0,)), ((), ())), preferred_element_type=jnp.float32)


def scatter_blocks(place, total, outs, n):
    for d in range(4):
        for e in range(4):
            s1, s2 = (place[0] + d) & 3, (place[1] + e) & 3
            skew = (s1 + s2) & 3
            rows = pl.ds(pl.multiple_of(jnp.where(place[3] == 0, s1, skew) * T, T), T)
            columns = pl.ds(pl.multiple_of(jnp.where(place[3] == 0, skew, s2) * T, T), T)
            outs[d][e, n] = total[rows, columns].astype(outs[d].dtype)


def block_shapes(count):
    return [jax.ShapeDtypeStruct((4, count, T, T), jnp.float32 if d == 0 else jnp.bfloat16) for d in range(4)]


def own_kernel(place, frequencies, own, gaps, scaled, *rest):
    outs, total = rest[:4], rest[4]
    gap = jnp.broadcast_to(gaps[...], (8, gaps.shape[1]))
    weights = [(4.0 * gap / (gap * gap + frequencies[f] * frequencies[f])).T[:, 0:1] for f in range(FREQ)]
    for h in range(2):
        for f in range(FREQ):
            part = 2 * f + h
            scaled[part] = (own[:, 512 * h : 512 * (h + 1)].astype(jnp.float32) * weights[f]).astype(jnp.bfloat16)
            total[...] = product(own[:, :512], scaled[part])
            scatter_blocks(place, total, outs, f * 3 + h)
            if h == 1:
                total[...] = product(own[:, 512:], scaled[part])
                scatter_blocks(place, total, outs, f * 3 + 2)


def own_products(place, frequencies, own, gaps):
    rows = own.shape[0]
    return call(
        own_kernel,
        [jax.ShapeDtypeStruct((4, rows, 512), jnp.bfloat16)] + block_shapes(10),
        [place, frequencies],
        [own, gaps.reshape(1, rows)],
        [pltpu.VMEM((512, 512), jnp.float32)],
        flops=2 * 6 * 512 * 512 * rows,
        name="own_products",
    )


def mate_kernel(place, other, scaled, *rest):
    outs, total = rest[4:8], rest[8]

    def step(t, _):
        columns = pl.ds(pl.multiple_of(t // 2 * 512, 512), 512)
        total[...] = product(other[:, columns], scaled[2 * place[3] + t % 2])
        scatter_blocks(place, total, outs, 6 + t)
        return 0

    lax.fori_loop(0, 4, step, 0)


def mate_products(place, other, scaled, blocks):
    return call(
        mate_kernel,
        block_shapes(10),
        [place],
        [other, scaled, *blocks],
        [pltpu.VMEM((512, 512), jnp.float32)],
        flops=2 * 4 * 512 * 512 * other.shape[0],
        name="mate_products",
        aliases={3 + d: d for d in range(4)},
    )


def far_kernel(place, other, scaled, *rest):
    outs, total = rest[:4], rest[4]

    def step(t, _):
        total[...] = product(other[...], scaled[t])
        scatter_blocks(place, total, outs, t)
        return 0

    lax.fori_loop(0, 4, step, 0)


def far_products(place, other, scaled):
    return call(
        far_kernel,
        block_shapes(4),
        [place],
        [other, scaled],
        [pltpu.VMEM((512, 512), jnp.float32)],
        flops=2 * 4 * 512 * 512 * other.shape[0],
        name="far_products",
    )


def seal(outs, largest):
    divisor = jnp.clip(jnp.broadcast_to(largest, (16, T)) * 2.0**5, 2.0**-17, 2.0**15)
    divisor = divisor.astype(jnp.bfloat16).astype(jnp.float32)
    factor = (2.0**19 / divisor)[0:1]
    for out in outs:
        for row in range(0, out.shape[0] - 16, T):
            out[row : row + T] = out[row : row + T] * factor
        out[out.shape[0] - 16 :] = divisor


def sealed(count):
    return floats(count * T + 16, T)


def opened(value, start, count):
    end = start + count * T
    return value[start:end].astype(jnp.float32) * (value[end : end + 1].astype(jnp.float32) * 2.0**-19)


def halved(values):
    return [v.astype(jnp.float16) for v in values]


def largest_of(values):
    peak = functools.reduce(jnp.maximum, [jnp.abs(v) for v in values])
    return jnp.max(jnp.max(peak, axis=0, keepdims=True), axis=1, keepdims=True)


def first_sum_kernel(kept, a, b, c, *outs):
    peak = jnp.zeros((T, T), jnp.float32)
    for e in range(4):
        for n in range(kept.shape[1]):
            value = kept[e, n] + (a[e, n].astype(jnp.float32) + b[e, n].astype(jnp.float32)) + c[e, n].astype(jnp.float32)
            outs[e][n * T : (n + 1) * T] = value
            if e > 0:
                peak = jnp.maximum(peak, jnp.abs(value))
    seal(outs[1:], largest_of([peak]))


def first_sum(kept, a, b, c):
    count = kept.shape[1]
    kept, *send = call(
        first_sum_kernel,
        [floats(count * T, T)] + [sealed(count)] * 3,
        [],
        [kept, a, b, c],
        flops=20 * count * T * T,
        name="first_sum",
    )
    return kept, halved(send)


def seal_kernel(value, out):
    peak = jnp.zeros((T, T), jnp.float32)
    for row in range(0, value.shape[0], T):
        out[row : row + T] = value[row : row + T]
        peak = jnp.maximum(peak, jnp.abs(value[row : row + T]))
    seal([out], largest_of([peak]))


def across(value, at_home):
    pairs = [(s, d) for s, d in shift_perm(dy=1) if ((d >> 6) == (d & 3) >> 1) == at_home]
    count = value.shape[0] // T
    send = call(seal_kernel, [sealed(count)], [], [value], flops=2 * count * T * T, name="seal")
    return value + opened(permute(halved(send)[0], pairs), 0, count)


def pack_kernel(place, near, twin, far, *rest):
    outs, ready = rest[:4], rest[4]
    at_home = place[4] == 1
    block = lambda part, n: part[n * T : (n + 1) * T]

    @pl.when(at_home)
    def _():
        core = place[3]
        for f in range(FREQ):
            low, both, high = (block(near, 3 * f + j) for j in range(3))
            ready[0, f, 0] = low
            ready[0, f, 1] = both
            ready[1, f, 0] = both.T
            ready[1, f, 1] = high.T
        for k in range(2):
            for h in range(2):
                ready[2 + k, core, h] = block(near, 6 + 2 * h + k).T
                ready[2 + k, 1 - core, h] = block(twin, 2 * k + h)

    @pl.when(jnp.logical_not(at_home))
    def _():
        for half in range(2):
            for f in range(FREQ):
                for h in range(2):
                    value = block(far, 4 * half + 2 * f + h)
                    ready[half, f, h] = value
                    ready[2 + h, f, half] = value.T

    peak = jnp.zeros((T, T), jnp.float32)
    for k in range(4):
        for f in range(FREQ):
            for h in range(2):
                value = ready[place[5 + k], f, h]
                row = (2 * f + h) * T
                outs[k][row : row + T] = value
                peak = jnp.maximum(peak, jnp.abs(value))
    seal(outs, largest_of([peak]))


def pack(place, *arrays):
    return halved(
        call(
            pack_kernel,
            [sealed(2 * FREQ)] * 4,
            [place],
            arrays,
            [pltpu.VMEM((4, FREQ, 2, T, T), jnp.float32)],
            flops=2**20,
            name="pack",
        )
    )


def unpack_kernel(place, a, b, c, d, out):
    for k, arrived in enumerate((a, b, c, d)):
        for f in range(FREQ):
            for h in range(2):
                out[:, f, pl.ds(pl.multiple_of(512 * h + place[9 + k] * T, T), T)] = arrived[(2 * f + h) * T : (2 * f + h + 1) * T]


def unpack(place, arrived):
    arrived = [opened(v, 0, 2 * FREQ) for v in arrived]
    return call(unpack_kernel, [floats(T, FREQ, 1024)], [place], arrived, flops=2**18, name="unpack")[0]


def after(value, earlier):
    return value if earlier is None else lax.optimization_barrier((value, earlier))[0]


def send_first(send, earlier):
    return [permute(after(v, w), shift_perm(d1=d + 1)) for d, (v, w) in enumerate(zip(send, earlier))]


def send_second(send, earlier):
    return [permute(after(v, w), shift_perm(d2=e + 1)) for e, (v, w) in enumerate(zip(send, earlier))]


def on_device(own, energy_gaps, frequencies):
    blk, grp = lax.axis_index("blk"), lax.axis_index("grp")
    x, z, y_hi, core = blk & 3, (blk >> 2) & 3, blk >> 4, grp & 1
    perms, sent, filled = rounds()
    tables = lax.dynamic_index_in_dim(jnp.asarray(np.concatenate([sent, filled]).T), blk * 4 + grp, 0, keepdims=False)
    home = jnp.where(y_hi == grp >> 1, 1, 0)
    here = jnp.stack([jnp.where(core == 0, x, z), jnp.where(core == 0, z, x), y_hi, core, home]).astype(jnp.int32)
    place = jnp.concatenate([here, tables])

    swap, far_perm = group_perm(lambda g: g ^ 1), group_perm(lambda g: FAR[g])
    low = own[:, :512]
    own, low = lax.optimization_barrier((own, low))
    other = permute(own, swap)
    far0 = permute(low, far_perm)

    scaled, *blocks = own_products(here, frequencies, own, energy_gaps)
    near, *send = mate_products(place, other, scaled, blocks)
    high = after(own, near)[:, 512:]
    far1 = permute(after(high, far0), far_perm)
    near_sent = send_first(send, [None, None, None])
    sum0, *send = far_products(place, far0, scaled)
    sum0_sent = send_first(send, near_sent)
    near, send = first_sum(near, *near_sent)
    near_sent = send_second(send, [sum0_sent[0], sum0_sent[1], sum0_sent[2]])
    sum0, send0 = first_sum(sum0, *sum0_sent)
    sum1, *send = far_products(place, far1, scaled)
    sum1_sent = send_first(send, near_sent)
    sum1, send1 = first_sum(sum1, *sum1_sent)
    for v in near_sent:
        near = near + opened(v, 0, 10)
    near = across(after(near, sum1_sent[2]), True)
    twin = permute(near[6 * T :], swap)
    for v in send_second([jnp.concatenate(v) for v in zip(send0, send1)], [None]*3):
        sum0 = sum0 + opened(v, 0, 4)
        sum1 = sum1 + opened(v, 4 * T + 16, 4)
    far = across(jnp.concatenate([sum0, sum1]), False)
    packed = pack(place, near, twin, far)
    return unpack(place, [permute(v, p) for v, p in zip(packed, perms)])


def solution(mesh):
    in_specs = (P("blk", "grp"), P("blk"), P())
    out_specs = P("blk", None, "grp")
    return jax.shard_map(
        on_device, mesh=mesh, in_specs=in_specs, out_specs=out_specs, check_vma=False
    )
```

```python
import functools

import jax
import jax.numpy as jnp
import numpy as np
from jax import lax
from jax.experimental import pallas as pl
from jax.experimental.pallas import tpu as pltpu
from jax.sharding import PartitionSpec as P

AXES = ("blk", "grp")
FREQ = 2
T = 128
FAR = (2, 3, 1, 0)
VMEM = 8 * 1024 * 1024


def parts_of(d):
    x, z, y_hi, grp = (d >> 2) & 3, (d >> 4) & 3, d >> 6, d & 3
    return (y_hi, x, z, grp) if grp & 1 == 0 else (y_hi, z, x, grp)


def device(y_hi, s1, s2, grp):
    x, z = (s1, s2) if grp & 1 == 0 else (s2, s1)
    return (((y_hi * 4 + z) * 4 + x) << 2) + grp


def shift_perm(d1=0, d2=0, dy=0):
    pairs = []
    for d in range(128):
        y_hi, s1, s2, grp = parts_of(d)
        pairs.append((d, device(y_hi ^ dy, (s1 + d1) & 3, (s2 + d2) & 3, grp)))
    return pairs


def group_perm(source):
    return [(blk * 4 + source(grp), blk * 4 + grp) for blk in range(32) for grp in range(4)]


def block_of(core, s1, s2):
    skew = (s1 + s2) & 3
    return (s1, skew) if core == 0 else (skew, s2)


def messages(d):
    y_hi, s1, s2, g = parts_of(d)
    s1, s2 = block_of(g & 1, s1, s2)
    row = lambda group, half, block, grp: (8 * group + 4 * half + block) * 4 + grp
    if y_hi == g >> 1:
        return [
            (row(g, 0, s1, g), s2),
            (row(g, 1, s2, g), s1),
            (row(g, 0, s2, g ^ 1), s1),
            (row(g, 1, s2, g ^ 1), s1),
        ]
    far = FAR[g]
    return [
        (row(far, 0, s1, g), s2),
        (row(far, 1, s1, g), s2),
        (row(g, 0, s2, far), s1),
        (row(g, 1, s2, far), s1),
    ]


@functools.cache
def rounds():
    perms, sent, filled = [], np.zeros((4, 128), np.int32), np.zeros((4, 128), np.int32)
    for k in range(4):
        pairs = []
        for d in range(128):
            sent[k, d] = ((d >> 4) & 3) ^ k
            to, slot = messages(d)[sent[k, d]]
            filled[k, to] = slot
            pairs.append((d, to))
        perms.append(pairs)
    return perms, sent, filled


def permute(value, pairs):
    return lax.ppermute(value, AXES, pairs)


def call(kernel, out_shape, scalars, arrays, scratch=(), flops=0, name=None, aliases=()):
    vmem, smem = pl.BlockSpec(memory_space=pltpu.VMEM), pl.BlockSpec(memory_space=pltpu.SMEM)
    size = 0
    return pl.pallas_call(
        kernel,
        out_shape=out_shape,
        in_specs=[smem] * len(scalars) + [vmem] * len(arrays),
        out_specs=[vmem] * len(out_shape),
        scratch_shapes=list(scratch),
        input_output_aliases=dict(aliases),
        compiler_params=pltpu.CompilerParams(vmem_limit_bytes=VMEM),
        cost_estimate=pl.CostEstimate(flops=flops, bytes_accessed=size, transcendentals=0),
        name=name,
    )(*scalars, *arrays)


def floats(*shape):
    return jax.ShapeDtypeStruct(shape, jnp.float32)


def product(lhs, rhs):
    return lax.dot_general(lhs, rhs, (((0,), (0,)), ((), ())), preferred_element_type=jnp.float32)


def scatter_blocks(place, total, outs, n):
    for d in range(4):
        for e in range(4):
            s1, s2 = (place[0] + d) & 3, (place[1] + e) & 3
            skew = (s1 + s2) & 3
            rows = pl.ds(pl.multiple_of(jnp.where(place[3] == 0, s1, skew) * T, T), T)
            columns = pl.ds(pl.multiple_of(jnp.where(place[3] == 0, skew, s2) * T, T), T)
            outs[d][e, n] = total[rows, columns].astype(outs[d].dtype)


def block_shapes(count):
    return [jax.ShapeDtypeStruct((4, count, T, T), jnp.float32 if d == 0 else jnp.bfloat16) for d in range(4)]


def own_kernel(place, frequencies, own, gaps, scaled, *rest):
    outs, total = rest[:4], rest[4]
    gap = jnp.broadcast_to(gaps[...], (8, gaps.shape[1]))
    weights = [(4.0 * gap / (gap * gap + frequencies[f] * frequencies[f])).T[:, 0:1] for f in range(FREQ)]
    for h in range(2):
        for f in range(FREQ):
            part = 2 * f + h
            scaled[part] = (own[:, 512 * h : 512 * (h + 1)].astype(jnp.float32) * weights[f]).astype(jnp.bfloat16)
            total[...] = product(own[:, :512], scaled[part])
            scatter_blocks(place, total, outs, f * 3 + h)
            if h == 1:
                total[...] = product(own[:, 512:], scaled[part])
                scatter_blocks(place, total, outs, f * 3 + 2)


def own_products(place, frequencies, own, gaps):
    rows = own.shape[0]
    return call(
        own_kernel,
        [jax.ShapeDtypeStruct((4, rows, 512), jnp.bfloat16)] + block_shapes(10),
        [place, frequencies],
        [own, gaps.reshape(1, rows)],
        [pltpu.VMEM((512, 512), jnp.float32)],
        flops=2 * 6 * 512 * 512 * rows,
        name="own_products",
    )


def mate_kernel(place, other, scaled, *rest):
    outs, total = rest[4:8], rest[8]

    for t in range(4):
        half = slice(t // 2 * 512, t // 2 * 512 + 512)
        total[...] = product(other[:, half], scaled[2 * place[3] + t % 2])
        scatter_blocks(place, total, outs, 6 + t)


def mate_products(place, other, scaled, blocks):
    return call(
        mate_kernel,
        block_shapes(10),
        [place],
        [other, scaled, *blocks],
        [pltpu.VMEM((512, 512), jnp.float32)],
        flops=2 * 4 * 512 * 512 * other.shape[0],
        name="mate_products",
        aliases={3 + d: d for d in range(4)},
    )


def far_kernel(place, other, scaled, *rest):
    outs, total = rest[:4], rest[4]

    def step(t, _):
        total[...] = product(other[...], scaled[t])
        scatter_blocks(place, total, outs, t)
        return 0

    lax.fori_loop(0, 4, step, 0)


def far_products(place, other, scaled):
    return call(
        far_kernel,
        block_shapes(4),
        [place],
        [other, scaled],
        [pltpu.VMEM((512, 512), jnp.float32)],
        flops=2 * 4 * 512 * 512 * other.shape[0],
        name="far_products",
    )


def seal(outs, largest):
    divisor = jnp.clip(jnp.broadcast_to(largest, (16, T)) * 2.0**5, 2.0**-17, 2.0**15)
    divisor = divisor.astype(jnp.bfloat16).astype(jnp.float32)
    factor = (2.0**19 / divisor)[0:1]
    for out in outs:
        for row in range(0, out.shape[0] - 16, T):
            out[row : row + T] = out[row : row + T] * factor
        out[out.shape[0] - 16 :] = divisor


def sealed(count):
    return floats(count * T + 16, T)


def opened(value, start, count):
    end = start + count * T
    return value[start:end].astype(jnp.float32) * (value[end : end + 1].astype(jnp.float32) * 2.0**-19)


def halved(values):
    return [v.astype(jnp.float16) for v in values]


def largest_of(values):
    peak = functools.reduce(jnp.maximum, [jnp.abs(v) for v in values])
    return jnp.max(jnp.max(peak, axis=0, keepdims=True), axis=1, keepdims=True)


def first_sum_kernel(kept, a, b, c, *outs):
    peak = jnp.zeros((T, T), jnp.float32)
    for e in range(4):
        for n in range(kept.shape[1]):
            value = kept[e, n] + (a[e, n].astype(jnp.float32) + b[e, n].astype(jnp.float32)) + c[e, n].astype(jnp.float32)
            outs[e][n * T : (n + 1) * T] = value
            if e > 0:
                peak = jnp.maximum(peak, jnp.abs(value))
    seal(outs[1:], largest_of([peak]))


def first_sum(kept, a, b, c):
    count = kept.shape[1]
    kept, *send = call(
        first_sum_kernel,
        [floats(count * T, T)] + [sealed(count)] * 3,
        [],
        [kept, a, b, c],
        flops=20 * count * T * T,
        name="first_sum",
    )
    return kept, halved(send)


def seal_kernel(value, out):
    peak = jnp.zeros((T, T), jnp.float32)
    for row in range(0, value.shape[0], T):
        out[row : row + T] = value[row : row + T]
        peak = jnp.maximum(peak, jnp.abs(value[row : row + T]))
    seal([out], largest_of([peak]))


def across(value, at_home):
    pairs = [(s, d) for s, d in shift_perm(dy=1) if ((d >> 6) == (d & 3) >> 1) == at_home]
    count = value.shape[0] // T
    send = call(seal_kernel, [sealed(count)], [], [value], flops=2 * count * T * T, name="seal")
    return value + opened(permute(halved(send)[0], pairs), 0, count)


def pack_kernel(place, near, twin, far, *rest):
    outs, ready = rest[:4], rest[4]
    at_home = place[4] == 1
    block = lambda part, n: part[n * T : (n + 1) * T]

    @pl.when(at_home)
    def _():
        core = place[3]
        for f in range(FREQ):
            low, both, high = (block(near, 3 * f + j) for j in range(3))
            ready[0, f, 0] = low
            ready[0, f, 1] = both
            ready[1, f, 0] = both.T
            ready[1, f, 1] = high.T
        for k in range(2):
            for h in range(2):
                ready[2 + k, core, h] = block(near, 6 + 2 * h + k).T
                ready[2 + k, 1 - core, h] = block(twin, 2 * k + h)

    @pl.when(jnp.logical_not(at_home))
    def _():
        for half in range(2):
            for f in range(FREQ):
                for h in range(2):
                    value = block(far, 4 * half + 2 * f + h)
                    ready[half, f, h] = value
                    ready[2 + h, f, half] = value.T

    peak = jnp.zeros((T, T), jnp.float32)
    for k in range(4):
        for f in range(FREQ):
            for h in range(2):
                value = ready[place[5 + k], f, h]
                row = (2 * f + h) * T
                outs[k][row : row + T] = value
                peak = jnp.maximum(peak, jnp.abs(value))
    seal(outs, largest_of([peak]))


def pack(place, *arrays):
    return halved(
        call(
            pack_kernel,
            [sealed(2 * FREQ)] * 4,
            [place],
            arrays,
            [pltpu.VMEM((4, FREQ, 2, T, T), jnp.float32)],
            flops=2**20,
            name="pack",
        )
    )


def unpack_kernel(place, a, b, c, d, out):
    for k, arrived in enumerate((a, b, c, d)):
        for f in range(FREQ):
            for h in range(2):
                out[:, f, pl.ds(pl.multiple_of(512 * h + place[9 + k] * T, T), T)] = arrived[(2 * f + h) * T : (2 * f + h + 1) * T]


def unpack(place, arrived):
    arrived = [opened(v, 0, 2 * FREQ) for v in arrived]
    return call(unpack_kernel, [floats(T, FREQ, 1024)], [place], arrived, flops=2**18, name="unpack")[0]


def after(value, earlier):
    return value if earlier is None else lax.optimization_barrier((value, earlier))[0]


def send_first(send, earlier):
    return [permute(after(v, w), shift_perm(d1=d + 1)) for d, (v, w) in enumerate(zip(send, earlier))]


def send_second(send, earlier):
    return [permute(after(v, w), shift_perm(d2=e + 1)) for e, (v, w) in enumerate(zip(send, earlier))]


def on_device(own, energy_gaps, frequencies):
    blk, grp = lax.axis_index("blk"), lax.axis_index("grp")
    x, z, y_hi, core = blk & 3, (blk >> 2) & 3, blk >> 4, grp & 1
    perms, sent, filled = rounds()
    tables = lax.dynamic_index_in_dim(jnp.asarray(np.concatenate([sent, filled]).T), blk * 4 + grp, 0, keepdims=False)
    home = jnp.where(y_hi == grp >> 1, 1, 0)
    here = jnp.stack([jnp.where(core == 0, x, z), jnp.where(core == 0, z, x), y_hi, core, home]).astype(jnp.int32)
    place = jnp.concatenate([here, tables])

    swap, far_perm = group_perm(lambda g: g ^ 1), group_perm(lambda g: FAR[g])
    low = own[:, :512]
    own, low = lax.optimization_barrier((own, low))
    other = permute(own, swap)
    far0 = permute(low, far_perm)

    scaled, *blocks = own_products(here, frequencies, own, energy_gaps)
    near, *send = mate_products(place, other, scaled, blocks)
    high = after(own, near)[:, 512:]
    far1 = permute(after(high, far0), far_perm)
    near_sent = send_first(send, [None, None, None])
    sum0, *send = far_products(place, far0, scaled)
    sum0_sent = send_first(send, near_sent)
    near, send = first_sum(near, *near_sent)
    near_sent = send_second(send, [sum0_sent[0], sum0_sent[1], sum0_sent[2]])
    sum0, send0 = first_sum(sum0, *sum0_sent)
    sum1, *send = far_products(place, far1, scaled)
    sum1_sent = send_first(send, near_sent)
    sum1, send1 = first_sum(sum1, *sum1_sent)
    for v in near_sent:
        near = near + opened(v, 0, 10)
    near = across(after(near, sum1_sent[2]), True)
    twin = permute(near[6 * T :], swap)
    for v in send_second([jnp.concatenate(v) for v in zip(send0, send1)], [None]*3):
        sum0 = sum0 + opened(v, 0, 4)
        sum1 = sum1 + opened(v, 4 * T + 16, 4)
    far = across(jnp.concatenate([sum0, sum1]), False)
    packed = pack(place, near, twin, far)
    return unpack(place, [permute(v, p) for v, p in zip(packed, perms)])


def solution(mesh):
    in_specs = (P("blk", "grp"), P("blk"), P())
    out_specs = P("blk", None, "grp")
    return jax.shard_map(
        on_device, mesh=mesh, in_specs=in_specs, out_specs=out_specs, check_vma=False
    )
```

```python
import functools

import jax
import jax.numpy as jnp
import numpy as np
from jax import lax
from jax.experimental import pallas as pl
from jax.experimental.pallas import tpu as pltpu
from jax.sharding import PartitionSpec as P

AXES = ("blk", "grp")
FREQ = 2
T = 128
FAR = (2, 3, 1, 0)
VMEM = 8 * 1024 * 1024


def parts_of(d):
    x, z, y_hi, grp = (d >> 2) & 3, (d >> 4) & 3, d >> 6, d & 3
    return (y_hi, x, z, grp) if grp & 1 == 0 else (y_hi, z, x, grp)


def device(y_hi, s1, s2, grp):
    x, z = (s1, s2) if grp & 1 == 0 else (s2, s1)
    return (((y_hi * 4 + z) * 4 + x) << 2) + grp


def swap_perm(d1=0, d2=0, dy=0):
    pairs = []
    for d in range(128):
        y_hi, s1, s2, grp = parts_of(d)
        pairs.append((d, device(y_hi ^ dy, s1 ^ d1, s2 ^ d2, grp)))
    return pairs


def group_perm(source):
    return [(blk * 4 + source(grp), blk * 4 + grp) for blk in range(32) for grp in range(4)]


def block_of(core, s1, s2):
    skew = (s1 + s2) & 3
    return (s1, skew) if core == 0 else (skew, s2)


def messages(d):
    y_hi, s1, s2, g = parts_of(d)
    s1, s2 = block_of(g & 1, s1, s2)
    row = lambda group, half, block, grp: (8 * group + 4 * half + block) * 4 + grp
    if y_hi == g >> 1:
        return [
            (row(g, 0, s1, g), s2),
            (row(g, 1, s2, g), s1),
            (row(g, 0, s2, g ^ 1), s1),
            (row(g, 1, s2, g ^ 1), s1),
        ]
    far = FAR[g]
    return [
        (row(far, 0, s1, g), s2),
        (row(far, 1, s1, g), s2),
        (row(g, 0, s2, far), s1),
        (row(g, 1, s2, far), s1),
    ]


@functools.cache
def rounds():
    perms, sent, filled = [], np.zeros((4, 128), np.int32), np.zeros((4, 128), np.int32)
    for k in range(4):
        pairs = []
        for d in range(128):
            sent[k, d] = ((d >> 4) & 3) ^ k
            to, slot = messages(d)[sent[k, d]]
            filled[k, to] = slot
            pairs.append((d, to))
        perms.append(pairs)
    return perms, sent, filled


def permute(value, pairs):
    return lax.ppermute(value, AXES, pairs)


def call(kernel, out_shape, scalars, arrays, scratch=(), flops=0, name=None, aliases=()):
    vmem, smem = pl.BlockSpec(memory_space=pltpu.VMEM), pl.BlockSpec(memory_space=pltpu.SMEM)
    size = 0
    return pl.pallas_call(
        kernel,
        out_shape=out_shape,
        in_specs=[smem] * len(scalars) + [vmem] * len(arrays),
        out_specs=[vmem] * len(out_shape),
        scratch_shapes=list(scratch),
        input_output_aliases=dict(aliases),
        compiler_params=pltpu.CompilerParams(vmem_limit_bytes=VMEM),
        cost_estimate=pl.CostEstimate(flops=flops, bytes_accessed=size, transcendentals=0),
        name=name,
    )(*scalars, *arrays)


def floats(*shape):
    return jax.ShapeDtypeStruct(shape, jnp.float32)


def product(lhs, rhs):
    return lax.dot_general(lhs, rhs, (((0,), (0,)), ((), ())), preferred_element_type=jnp.float32)


def scatter_blocks(place, total, outs, n):
    for d in range(4):
        for e in range(4):
            s1, s2 = place[0] ^ d, place[1] ^ e
            skew = (s1 + s2) & 3
            rows = pl.ds(pl.multiple_of(jnp.where(place[3] == 0, s1, skew) * T, T), T)
            columns = pl.ds(pl.multiple_of(jnp.where(place[3] == 0, skew, s2) * T, T), T)
            outs[d][e, n] = total[rows, columns].astype(outs[d].dtype)


def block_shapes(count):
    return [jax.ShapeDtypeStruct((4, count, T, T), jnp.float32 if d == 0 else jnp.bfloat16) for d in range(4)]


def own_kernel(place, frequencies, own, gaps, scaled, *rest):
    outs, total = rest[:4], rest[4]
    gap = jnp.broadcast_to(gaps[...], (8, gaps.shape[1]))
    weights = [(4.0 * gap / (gap * gap + frequencies[f] * frequencies[f])).T[:, 0:1] for f in range(FREQ)]
    for h in range(2):
        for f in range(FREQ):
            part = 2 * f + h
            scaled[part] = (own[:, 512 * h : 512 * (h + 1)].astype(jnp.float32) * weights[f]).astype(jnp.bfloat16)
            total[...] = product(own[:, :512], scaled[part])
            scatter_blocks(place, total, outs, f * 3 + h)
            if h == 1:
                total[...] = product(own[:, 512:], scaled[part])
                scatter_blocks(place, total, outs, f * 3 + 2)


def own_products(place, frequencies, own, gaps):
    rows = own.shape[0]
    return call(
        own_kernel,
        [jax.ShapeDtypeStruct((4, rows, 512), jnp.bfloat16)] + block_shapes(10),
        [place, frequencies],
        [own, gaps.reshape(1, rows)],
        [pltpu.VMEM((512, 512), jnp.float32)],
        flops=2 * 6 * 512 * 512 * rows,
        name="own_products",
    )


def mate_kernel(place, other, scaled, *rest):
    outs, total = rest[4:8], rest[8]

    for t in range(4):
        half = slice(t // 2 * 512, t // 2 * 512 + 512)
        total[...] = product(other[:, half], scaled[2 * place[3] + t % 2])
        scatter_blocks(place, total, outs, 6 + t)


def mate_products(place, other, scaled, blocks):
    return call(
        mate_kernel,
        block_shapes(10),
        [place],
        [other, scaled, *blocks],
        [pltpu.VMEM((512, 512), jnp.float32)],
        flops=2 * 4 * 512 * 512 * other.shape[0],
        name="mate_products",
        aliases={3 + d: d for d in range(4)},
    )


def far_kernel(place, other, scaled, *rest):
    outs, total = rest[:4], rest[4]

    def step(t, _):
        total[...] = product(other[...], scaled[t])
        scatter_blocks(place, total, outs, t)
        return 0

    lax.fori_loop(0, 4, step, 0)


def far_products(place, other, scaled):
    return call(
        far_kernel,
        block_shapes(4),
        [place],
        [other, scaled],
        [pltpu.VMEM((512, 512), jnp.float32)],
        flops=2 * 4 * 512 * 512 * other.shape[0],
        name="far_products",
    )


def seal(outs, largest):
    divisor = jnp.clip(jnp.broadcast_to(largest, (16, T)) * 2.0**5, 2.0**-17, 2.0**15)
    divisor = divisor.astype(jnp.bfloat16).astype(jnp.float32)
    factor = (2.0**19 / divisor)[0:1]
    for out in outs:
        for row in range(0, out.shape[0] - 16, T):
            out[row : row + T] = out[row : row + T] * factor
        out[out.shape[0] - 16 :] = divisor


def sealed(count):
    return floats(count * T + 16, T)


def opened(value, start, count):
    end = start + count * T
    return value[start:end].astype(jnp.float32) * (value[end : end + 1].astype(jnp.float32) * 2.0**-19)


def halved(values):
    return [v.astype(jnp.float16) for v in values]


def largest_of(values):
    peak = functools.reduce(jnp.maximum, [jnp.abs(v) for v in values])
    return jnp.max(jnp.max(peak, axis=0, keepdims=True), axis=1, keepdims=True)


def first_sum_kernel(kept, a, b, c, *outs):
    peak = jnp.zeros((T, T), jnp.float32)
    for e in range(4):
        for n in range(kept.shape[1]):
            value = kept[e, n] + (a[e, n].astype(jnp.float32) + b[e, n].astype(jnp.float32)) + c[e, n].astype(jnp.float32)
            outs[e][n * T : (n + 1) * T] = value
            if e > 0:
                peak = jnp.maximum(peak, jnp.abs(value))
    seal(outs[1:], largest_of([peak]))


def first_sum(kept, a, b, c):
    count = kept.shape[1]
    kept, *send = call(
        first_sum_kernel,
        [floats(count * T, T)] + [sealed(count)] * 3,
        [],
        [kept, a, b, c],
        flops=20 * count * T * T,
        name="first_sum",
    )
    return kept, halved(send)


def seal_kernel(value, out):
    peak = jnp.zeros((T, T), jnp.float32)
    for row in range(0, value.shape[0], T):
        out[row : row + T] = value[row : row + T]
        peak = jnp.maximum(peak, jnp.abs(value[row : row + T]))
    seal([out], largest_of([peak]))


def across(value, at_home):
    pairs = [(s, d) for s, d in swap_perm(dy=1) if ((d >> 6) == (d & 3) >> 1) == at_home]
    count = value.shape[0] // T
    send = call(seal_kernel, [sealed(count)], [], [value], flops=2 * count * T * T, name="seal")
    return value + opened(permute(halved(send)[0], pairs), 0, count)


def pack_kernel(place, near, twin, far, *rest):
    outs, ready = rest[:4], rest[4]
    at_home = place[4] == 1
    block = lambda part, n: part[n * T : (n + 1) * T]

    @pl.when(at_home)
    def _():
        core = place[3]
        for f in range(FREQ):
            low, both, high = (block(near, 3 * f + j) for j in range(3))
            ready[0, f, 0] = low
            ready[0, f, 1] = both
            ready[1, f, 0] = both.T
            ready[1, f, 1] = high.T
        for k in range(2):
            for h in range(2):
                ready[2 + k, core, h] = block(near, 6 + 2 * h + k).T
                ready[2 + k, 1 - core, h] = block(twin, 2 * k + h)

    @pl.when(jnp.logical_not(at_home))
    def _():
        for half in range(2):
            for f in range(FREQ):
                for h in range(2):
                    value = block(far, 4 * half + 2 * f + h)
                    ready[half, f, h] = value
                    ready[2 + h, f, half] = value.T

    peak = jnp.zeros((T, T), jnp.float32)
    for k in range(4):
        for f in range(FREQ):
            for h in range(2):
                value = ready[place[5 + k], f, h]
                row = (2 * f + h) * T
                outs[k][row : row + T] = value
                peak = jnp.maximum(peak, jnp.abs(value))
    seal(outs, largest_of([peak]))


def pack(place, *arrays):
    return halved(
        call(
            pack_kernel,
            [sealed(2 * FREQ)] * 4,
            [place],
            arrays,
            [pltpu.VMEM((4, FREQ, 2, T, T), jnp.float32)],
            flops=2**20,
            name="pack",
        )
    )


def unpack_kernel(place, a, b, c, d, out):
    for k, arrived in enumerate((a, b, c, d)):
        for f in range(FREQ):
            for h in range(2):
                out[:, f, pl.ds(pl.multiple_of(512 * h + place[9 + k] * T, T), T)] = arrived[(2 * f + h) * T : (2 * f + h + 1) * T]


def unpack(place, arrived):
    arrived = [opened(v, 0, 2 * FREQ) for v in arrived]
    return call(unpack_kernel, [floats(T, FREQ, 1024)], [place], arrived, flops=2**18, name="unpack")[0]


def after(value, earlier):
    return value if earlier is None else lax.optimization_barrier((value, earlier))[0]


def send_first(send, earlier):
    return [permute(after(v, w), swap_perm(d1=d + 1)) for d, (v, w) in enumerate(zip(send, earlier))]


def send_second(send, earlier):
    return [permute(after(v, w), swap_perm(d2=e + 1)) for e, (v, w) in enumerate(zip(send, earlier))]


def on_device(own, energy_gaps, frequencies):
    blk, grp = lax.axis_index("blk"), lax.axis_index("grp")
    x, z, y_hi, core = blk & 3, (blk >> 2) & 3, blk >> 4, grp & 1
    perms, sent, filled = rounds()
    tables = lax.dynamic_index_in_dim(jnp.asarray(np.concatenate([sent, filled]).T), blk * 4 + grp, 0, keepdims=False)
    home = jnp.where(y_hi == grp >> 1, 1, 0)
    here = jnp.stack([jnp.where(core == 0, x, z), jnp.where(core == 0, z, x), y_hi, core, home]).astype(jnp.int32)
    place = jnp.concatenate([here, tables])

    swap, far_perm = group_perm(lambda g: g ^ 1), group_perm(lambda g: FAR[g])
    low = own[:, :512]
    own, low = lax.optimization_barrier((own, low))
    other = permute(own, swap)
    far0 = permute(low, far_perm)

    scaled, *blocks = own_products(here, frequencies, own, energy_gaps)
    near, *send = mate_products(place, other, scaled, blocks)
    high = after(own, near)[:, 512:]
    far1 = permute(after(high, far0), far_perm)
    near_sent = send_first(send, [None, None, None])
    sum0, *send = far_products(place, far0, scaled)
    sum0_sent = send_first(send, near_sent)
    near, send = first_sum(near, *near_sent)
    near_sent = send_second(send, [sum0_sent[0], sum0_sent[1], sum0_sent[2]])
    sum0, send0 = first_sum(sum0, *sum0_sent)
    sum1, *send = far_products(place, far1, scaled)
    sum1_sent = send_first(send, near_sent)
    sum1, send1 = first_sum(sum1, *sum1_sent)
    for v in near_sent:
        near = near + opened(v, 0, 10)
    near = across(after(near, sum1_sent[2]), True)
    twin = permute(near[6 * T :], swap)
    for v in send_second([jnp.concatenate(v) for v in zip(send0, send1)], [None]*3):
        sum0 = sum0 + opened(v, 0, 4)
        sum1 = sum1 + opened(v, 4 * T + 16, 4)
    far = across(jnp.concatenate([sum0, sum1]), False)
    packed = pack(place, near, twin, far)
    return unpack(place, [permute(v, p) for v, p in zip(packed, perms)])


def solution(mesh):
    in_specs = (P("blk", "grp"), P("blk"), P())
    out_specs = P("blk", None, "grp")
    return jax.shard_map(
        on_device, mesh=mesh, in_specs=in_specs, out_specs=out_specs, check_vma=False
    )
```

```python
import functools

import jax
import jax.numpy as jnp
import numpy as np
from jax import lax
from jax.experimental import pallas as pl
from jax.experimental.pallas import tpu as pltpu
from jax.sharding import PartitionSpec as P

AXES = ("blk", "grp")
FREQ = 2
T = 128
FAR = (2, 3, 1, 0)
VMEM = 8 * 1024 * 1024


def parts_of(d):
    x, z, y_hi, grp = (d >> 2) & 3, (d >> 4) & 3, d >> 6, d & 3
    return (y_hi, x, z, grp) if grp & 1 == 0 else (y_hi, z, x, grp)


def device(y_hi, s1, s2, grp):
    x, z = (s1, s2) if grp & 1 == 0 else (s2, s1)
    return (((y_hi * 4 + z) * 4 + x) << 2) + grp


def swap_perm(d1=0, d2=0, dy=0):
    pairs = []
    for d in range(128):
        y_hi, s1, s2, grp = parts_of(d)
        pairs.append((d, device(y_hi ^ dy, s1 ^ d1, s2 ^ d2, grp)))
    return pairs


def group_perm(source):
    return [(blk * 4 + source(grp), blk * 4 + grp) for blk in range(32) for grp in range(4)]


def block_of(core, s1, s2):
    skew = (s1 + s2) & 3
    return (s1, skew) if core == 0 else (skew, s2)


def messages(d):
    y_hi, s1, s2, g = parts_of(d)
    s1, s2 = block_of(g & 1, s1, s2)
    row = lambda group, half, block, grp: (8 * group + 4 * half + block) * 4 + grp
    if y_hi == g >> 1:
        return [
            (row(g, 0, s1, g), s2),
            (row(g, 1, s2, g), s1),
            (row(g, 0, s2, g ^ 1), s1),
            (row(g, 1, s2, g ^ 1), s1),
        ]
    far = FAR[g]
    return [
        (row(far, 0, s1, g), s2),
        (row(far, 1, s1, g), s2),
        (row(g, 0, s2, far), s1),
        (row(g, 1, s2, far), s1),
    ]


@functools.cache
def rounds():
    perms, sent, filled = [], np.zeros((4, 128), np.int32), np.zeros((4, 128), np.int32)
    for k in range(4):
        pairs = []
        for d in range(128):
            sent[k, d] = ((d >> 4) & 3) ^ k
            to, slot = messages(d)[sent[k, d]]
            filled[k, to] = slot
            pairs.append((d, to))
        perms.append(pairs)
    return perms, sent, filled


def permute(value, pairs):
    return lax.ppermute(value, AXES, pairs)


def call(kernel, out_shape, scalars, arrays, scratch=(), flops=0, name=None, aliases=()):
    vmem, smem = pl.BlockSpec(memory_space=pltpu.VMEM), pl.BlockSpec(memory_space=pltpu.SMEM)
    size = 0
    return pl.pallas_call(
        kernel,
        out_shape=out_shape,
        in_specs=[smem] * len(scalars) + [vmem] * len(arrays),
        out_specs=[vmem] * len(out_shape),
        scratch_shapes=list(scratch),
        input_output_aliases=dict(aliases),
        compiler_params=pltpu.CompilerParams(vmem_limit_bytes=VMEM),
        cost_estimate=pl.CostEstimate(flops=flops, bytes_accessed=size, transcendentals=0),
        name=name,
    )(*scalars, *arrays)


def floats(*shape):
    return jax.ShapeDtypeStruct(shape, jnp.float32)


def product(lhs, rhs):
    return lax.dot_general(lhs, rhs, (((0,), (0,)), ((), ())), preferred_element_type=jnp.float32)


def scatter_blocks(place, total, outs, n):
    for d in range(4):
        for e in range(4):
            s1, s2 = place[0] ^ d, place[1] ^ e
            skew = (s1 + s2) & 3
            rows = pl.ds(pl.multiple_of(jnp.where(place[3] == 0, s1, skew) * T, T), T)
            columns = pl.ds(pl.multiple_of(jnp.where(place[3] == 0, skew, s2) * T, T), T)
            outs[d][e, n] = total[rows, columns].astype(outs[d].dtype)


def block_shapes(count):
    return [jax.ShapeDtypeStruct((4, count, T, T), jnp.float32 if d == 0 else jnp.bfloat16) for d in range(4)]


def own_kernel(place, frequencies, own, gaps, scaled, *rest):
    outs, total = rest[:4], rest[4]
    gap = jnp.broadcast_to(gaps[...], (8, gaps.shape[1]))
    weights = [(4.0 * gap / (gap * gap + frequencies[f] * frequencies[f])).T[:, 0:1] for f in range(FREQ)]
    for h in range(2):
        for f in range(FREQ):
            part = 2 * f + h
            scaled[part] = (own[:, 512 * h : 512 * (h + 1)].astype(jnp.float32) * weights[f]).astype(jnp.bfloat16)
            total[...] = product(own[:, :512], scaled[part])
            scatter_blocks(place, total, outs, f * 3 + h)
            if h == 1:
                total[...] = product(own[:, 512:], scaled[part])
                scatter_blocks(place, total, outs, f * 3 + 2)


def own_products(place, frequencies, own, gaps):
    rows = own.shape[0]
    return call(
        own_kernel,
        [jax.ShapeDtypeStruct((4, rows, 512), jnp.bfloat16)] + block_shapes(10),
        [place, frequencies],
        [own, gaps.reshape(1, rows)],
        [pltpu.VMEM((512, 512), jnp.float32)],
        flops=2 * 6 * 512 * 512 * rows,
        name="own_products",
    )


def mate_kernel(place, other, scaled, *rest):
    outs, total = rest[4:8], rest[8]

    for t in range(4):
        half = slice(t // 2 * 512, t // 2 * 512 + 512)
        total[...] = product(other[:, half], scaled[2 * place[3] + t % 2])
        scatter_blocks(place, total, outs, 6 + t)


def mate_products(place, other, scaled, blocks):
    return call(
        mate_kernel,
        block_shapes(10),
        [place],
        [other, scaled, *blocks],
        [pltpu.VMEM((512, 512), jnp.float32)],
        flops=2 * 4 * 512 * 512 * other.shape[0],
        name="mate_products",
        aliases={3 + d: d for d in range(4)},
    )


def far_kernel(place, other, scaled, *rest):
    outs, total = rest[:4], rest[4]

    def step(t, _):
        total[...] = product(other[...], scaled[t])
        scatter_blocks(place, total, outs, t)
        return 0

    lax.fori_loop(0, 4, step, 0)


def early_kernel(other, scaled, out):
    for t in range(4):
        out[t] = product(other[...], scaled[t])


def early_products(other, scaled):
    columns = other.shape[1]
    flops = 2 * 4 * columns * 512 * other.shape[0]
    return call(early_kernel, [floats(4, columns, 512)], [], [other, scaled], flops=flops, name="early_products")[0]


def late_kernel(place, other, scaled, early, *rest):
    outs, total = rest[:4], rest[4]
    rows = early.shape[1]
    for t in range(4):
        total[:rows] = early[t]
        total[rows:] = product(other[...], scaled[t])
        scatter_blocks(place, total, outs, t)


def late_products(place, other, scaled, early):
    return call(
        late_kernel,
        block_shapes(4),
        [place],
        [other, scaled, early],
        [pltpu.VMEM((512, 512), jnp.float32)],
        flops=2 * 4 * 256 * 512 * other.shape[0],
        name="late_products",
    )


def far_products(place, other, scaled):
    return call(
        far_kernel,
        block_shapes(4),
        [place],
        [other, scaled],
        [pltpu.VMEM((512, 512), jnp.float32)],
        flops=2 * 4 * 512 * 512 * other.shape[0],
        name="far_products",
    )


def seal(outs, largest):
    divisor = jnp.clip(jnp.broadcast_to(largest, (16, T)) * 2.0**5, 2.0**-17, 2.0**15)
    divisor = divisor.astype(jnp.bfloat16).astype(jnp.float32)
    factor = (2.0**19 / divisor)[0:1]
    for out in outs:
        for row in range(0, out.shape[0] - 16, T):
            out[row : row + T] = out[row : row + T] * factor
        out[out.shape[0] - 16 :] = divisor


def sealed(count):
    return floats(count * T + 16, T)


def opened(value, start, count):
    end = start + count * T
    return value[start:end].astype(jnp.float32) * (value[end : end + 1].astype(jnp.float32) * 2.0**-19)


def halved(values):
    return [v.astype(jnp.float16) for v in values]


def largest_of(values):
    peak = functools.reduce(jnp.maximum, [jnp.abs(v) for v in values])
    return jnp.max(jnp.max(peak, axis=0, keepdims=True), axis=1, keepdims=True)


def first_sum_kernel(kept, a, b, c, *outs):
    peak = jnp.zeros((T, T), jnp.float32)
    for e in range(4):
        for n in range(kept.shape[1]):
            value = kept[e, n] + (a[e, n].astype(jnp.float32) + b[e, n].astype(jnp.float32)) + c[e, n].astype(jnp.float32)
            outs[e][n * T : (n + 1) * T] = value
            if e > 0:
                peak = jnp.maximum(peak, jnp.abs(value))
    seal(outs[1:], largest_of([peak]))


def first_sum(kept, a, b, c):
    count = kept.shape[1]
    kept, *send = call(
        first_sum_kernel,
        [floats(count * T, T)] + [sealed(count)] * 3,
        [],
        [kept, a, b, c],
        flops=20 * count * T * T,
        name="first_sum",
    )
    return kept, halved(send)


def seal_kernel(value, out):
    peak = jnp.zeros((T, T), jnp.float32)
    for row in range(0, value.shape[0], T):
        out[row : row + T] = value[row : row + T]
        peak = jnp.maximum(peak, jnp.abs(value[row : row + T]))
    seal([out], largest_of([peak]))


def across(value, at_home):
    pairs = [(s, d) for s, d in swap_perm(dy=1) if ((d >> 6) == (d & 3) >> 1) == at_home]
    count = value.shape[0] // T
    send = call(seal_kernel, [sealed(count)], [], [value], flops=2 * count * T * T, name="seal")
    return value + opened(permute(halved(send)[0], pairs), 0, count)


def pack_kernel(place, near, twin, far, *rest):
    outs, ready = rest[:4], rest[4]
    at_home = place[4] == 1
    block = lambda part, n: part[n * T : (n + 1) * T]

    @pl.when(at_home)
    def _():
        core = place[3]
        for f in range(FREQ):
            low, both, high = (block(near, 3 * f + j) for j in range(3))
            ready[0, f, 0] = low
            ready[0, f, 1] = both
            ready[1, f, 0] = both.T
            ready[1, f, 1] = high.T
        for k in range(2):
            for h in range(2):
                ready[2 + k, core, h] = block(near, 6 + 2 * h + k).T
                ready[2 + k, 1 - core, h] = block(twin, 2 * k + h)

    @pl.when(jnp.logical_not(at_home))
    def _():
        for half in range(2):
            for f in range(FREQ):
                for h in range(2):
                    value = block(far, 4 * half + 2 * f + h)
                    ready[half, f, h] = value
                    ready[2 + h, f, half] = value.T

    peak = jnp.zeros((T, T), jnp.float32)
    for k in range(4):
        for f in range(FREQ):
            for h in range(2):
                value = ready[place[5 + k], f, h]
                row = (2 * f + h) * T
                outs[k][row : row + T] = value
                peak = jnp.maximum(peak, jnp.abs(value))
    seal(outs, largest_of([peak]))


def pack(place, *arrays):
    return halved(
        call(
            pack_kernel,
            [sealed(2 * FREQ)] * 4,
            [place],
            arrays,
            [pltpu.VMEM((4, FREQ, 2, T, T), jnp.float32)],
            flops=2**20,
            name="pack",
        )
    )


def unpack_kernel(place, a, b, c, d, out):
    for k, arrived in enumerate((a, b, c, d)):
        for f in range(FREQ):
            for h in range(2):
                out[:, f, pl.ds(pl.multiple_of(512 * h + place[9 + k] * T, T), T)] = arrived[(2 * f + h) * T : (2 * f + h + 1) * T]


def unpack(place, arrived):
    arrived = [opened(v, 0, 2 * FREQ) for v in arrived]
    return call(unpack_kernel, [floats(T, FREQ, 1024)], [place], arrived, flops=2**18, name="unpack")[0]


def after(value, earlier):
    return value if earlier is None else lax.optimization_barrier((value, earlier))[0]


def send_first(send, earlier):
    return [permute(after(v, w), swap_perm(d1=d + 1)) for d, (v, w) in enumerate(zip(send, earlier))]


def send_second(send, earlier):
    return [permute(after(v, w), swap_perm(d2=e + 1)) for e, (v, w) in enumerate(zip(send, earlier))]


def on_device(own, energy_gaps, frequencies):
    blk, grp = lax.axis_index("blk"), lax.axis_index("grp")
    x, z, y_hi, core = blk & 3, (blk >> 2) & 3, blk >> 4, grp & 1
    perms, sent, filled = rounds()
    tables = lax.dynamic_index_in_dim(jnp.asarray(np.concatenate([sent, filled]).T), blk * 4 + grp, 0, keepdims=False)
    home = jnp.where(y_hi == grp >> 1, 1, 0)
    here = jnp.stack([jnp.where(core == 0, x, z), jnp.where(core == 0, z, x), y_hi, core, home]).astype(jnp.int32)
    place = jnp.concatenate([here, tables])

    swap, far_perm = group_perm(lambda g: g ^ 1), group_perm(lambda g: FAR[g])
    low = own[:, :512]
    own, low = lax.optimization_barrier((own, low))
    other = permute(own, swap)
    far0 = permute(low, far_perm)

    scaled, *blocks = own_products(here, frequencies, own, energy_gaps)
    near, *send = mate_products(place, other, scaled, blocks)
    rest = after(own, near)
    far1 = permute(after(rest[:, 512:768], far0), far_perm)
    near_sent = send_first(send, [None, None, None])
    sum0, *send = far_products(place, far0, scaled)
    far2 = permute(after(rest[:, 768:], sum0), far_perm)
    sum0_sent = send_first(send, near_sent)
    near, send = first_sum(near, *near_sent)
    near_sent = send_second(send, [sum0_sent[0], sum0_sent[1], sum0_sent[2]])
    sum0, send0 = first_sum(sum0, *sum0_sent)
    early = early_products(far1, scaled)
    sum1, *send = late_products(place, far2, scaled, early)
    sum1_sent = send_first(send, near_sent)
    sum1, send1 = first_sum(sum1, *sum1_sent)
    for v in near_sent:
        near = near + opened(v, 0, 10)
    near = across(after(near, sum1_sent[2]), True)
    twin = permute(near[6 * T :], swap)
    for v in send_second([jnp.concatenate(v) for v in zip(send0, send1)], [None]*3):
        sum0 = sum0 + opened(v, 0, 4)
        sum1 = sum1 + opened(v, 4 * T + 16, 4)
    far = across(jnp.concatenate([sum0, sum1]), False)
    packed = pack(place, near, twin, far)
    return unpack(place, [permute(v, p) for v, p in zip(packed, perms)])


def solution(mesh):
    in_specs = (P("blk", "grp"), P("blk"), P())
    out_specs = P("blk", None, "grp")
    return jax.shard_map(
        on_device, mesh=mesh, in_specs=in_specs, out_specs=out_specs, check_vma=False
    )
```

```python
import functools

import jax
import jax.numpy as jnp
import numpy as np
from jax import lax
from jax.experimental import pallas as pl
from jax.experimental.pallas import tpu as pltpu
from jax.sharding import PartitionSpec as P

AXES = ("blk", "grp")
FREQ = 2
T = 128
FAR = (2, 3, 1, 0)
VMEM = 8 * 1024 * 1024


def parts_of(d):
    x, z, y_hi, grp = (d >> 2) & 3, (d >> 4) & 3, d >> 6, d & 3
    return (y_hi, x, z, grp) if grp & 1 == 0 else (y_hi, z, x, grp)


def device(y_hi, s1, s2, grp):
    x, z = (s1, s2) if grp & 1 == 0 else (s2, s1)
    return (((y_hi * 4 + z) * 4 + x) << 2) + grp


def swap_perm(d1=0, d2=0, dy=0):
    pairs = []
    for d in range(128):
        y_hi, s1, s2, grp = parts_of(d)
        pairs.append((d, device(y_hi ^ dy, s1 ^ d1, s2 ^ d2, grp)))
    return pairs


def group_perm(source):
    return [(blk * 4 + source(grp), blk * 4 + grp) for blk in range(32) for grp in range(4)]


def block_of(core, s1, s2):
    skew = (s1 + s2) & 3
    return (s1, skew) if core == 0 else (skew, s2)


def messages(d):
    y_hi, s1, s2, g = parts_of(d)
    s1, s2 = block_of(g & 1, s1, s2)
    row = lambda group, half, block, grp: (8 * group + 4 * half + block) * 4 + grp
    if y_hi == g >> 1:
        return [
            (row(g, 0, s1, g), s2),
            (row(g, 1, s2, g), s1),
            (row(g, 0, s2, g ^ 1), s1),
            (row(g, 1, s2, g ^ 1), s1),
        ]
    far = FAR[g]
    return [
        (row(far, 0, s1, g), s2),
        (row(far, 1, s1, g), s2),
        (row(g, 0, s2, far), s1),
        (row(g, 1, s2, far), s1),
    ]


@functools.cache
def rounds():
    perms, sent, filled = [], np.zeros((4, 128), np.int32), np.zeros((4, 128), np.int32)
    for k in range(4):
        pairs = []
        for d in range(128):
            sent[k, d] = (0, 1, 3, 2)[((d >> 4) & 3) ^ k]
            to, slot = messages(d)[sent[k, d]]
            filled[k, to] = slot
            pairs.append((d, to))
        perms.append(pairs)
    return perms, sent, filled


def permute(value, pairs):
    return lax.ppermute(value, AXES, pairs)


def call(kernel, out_shape, scalars, arrays, scratch=(), flops=0, name=None, aliases=()):
    vmem, smem = pl.BlockSpec(memory_space=pltpu.VMEM), pl.BlockSpec(memory_space=pltpu.SMEM)
    size = 0
    return pl.pallas_call(
        kernel,
        out_shape=out_shape,
        in_specs=[smem] * len(scalars) + [vmem] * len(arrays),
        out_specs=[vmem] * len(out_shape),
        scratch_shapes=list(scratch),
        input_output_aliases=dict(aliases),
        compiler_params=pltpu.CompilerParams(vmem_limit_bytes=VMEM),
        cost_estimate=pl.CostEstimate(flops=flops, bytes_accessed=size, transcendentals=0),
        name=name,
    )(*scalars, *arrays)


def floats(*shape):
    return jax.ShapeDtypeStruct(shape, jnp.float32)


def product(lhs, rhs):
    return lax.dot_general(lhs, rhs, (((0,), (0,)), ((), ())), preferred_element_type=jnp.float32)


def scatter_blocks(place, total, outs, n):
    for d in range(4):
        for e in range(4):
            s1, s2 = place[0] ^ d, place[1] ^ e
            skew = (s1 + s2) & 3
            rows = pl.ds(pl.multiple_of(jnp.where(place[3] == 0, s1, skew) * T, T), T)
            columns = pl.ds(pl.multiple_of(jnp.where(place[3] == 0, skew, s2) * T, T), T)
            outs[d][e, n] = total[rows, columns].astype(outs[d].dtype)


def block_shapes(count):
    return [jax.ShapeDtypeStruct((4, count, T, T), jnp.float32 if d == 0 else jnp.bfloat16) for d in range(4)]


def own_kernel(place, frequencies, own, gaps, scaled, *rest):
    outs, total = rest[:4], rest[4]
    gap = jnp.broadcast_to(gaps[...], (8, gaps.shape[1]))
    weights = [(4.0 * gap / (gap * gap + frequencies[f] * frequencies[f])).T[:, 0:1] for f in range(FREQ)]
    for h in range(2):
        for f in range(FREQ):
            part = 2 * f + h
            scaled[part] = (own[:, 512 * h : 512 * (h + 1)].astype(jnp.float32) * weights[f]).astype(jnp.bfloat16)
            total[...] = product(own[:, :512], scaled[part])
            scatter_blocks(place, total, outs, f * 3 + h)
            if h == 1:
                total[...] = product(own[:, 512:], scaled[part])
                scatter_blocks(place, total, outs, f * 3 + 2)


def own_products(place, frequencies, own, gaps):
    rows = own.shape[0]
    return call(
        own_kernel,
        [jax.ShapeDtypeStruct((4, rows, 512), jnp.bfloat16)] + block_shapes(10),
        [place, frequencies],
        [own, gaps.reshape(1, rows)],
        [pltpu.VMEM((512, 512), jnp.float32)],
        flops=2 * 6 * 512 * 512 * rows,
        name="own_products",
    )


def mate_kernel(place, other, scaled, *rest):
    outs, total = rest[4:8], rest[8]

    for t in range(4):
        half = slice(t // 2 * 512, t // 2 * 512 + 512)
        total[...] = product(other[:, half], scaled[2 * place[3] + t % 2])
        scatter_blocks(place, total, outs, 6 + t)


def mate_products(place, other, scaled, blocks):
    return call(
        mate_kernel,
        block_shapes(10),
        [place],
        [other, scaled, *blocks],
        [pltpu.VMEM((512, 512), jnp.float32)],
        flops=2 * 4 * 512 * 512 * other.shape[0],
        name="mate_products",
        aliases={3 + d: d for d in range(4)},
    )


def far_kernel(place, other, scaled, *rest):
    outs, total = rest[:4], rest[4]

    def step(t, _):
        total[...] = product(other[...], scaled[t])
        scatter_blocks(place, total, outs, t)
        return 0

    lax.fori_loop(0, 4, step, 0)


def early_kernel(other, scaled, out):
    for t in range(4):
        out[t] = product(other[...], scaled[t])


def early_products(other, scaled):
    columns = other.shape[1]
    flops = 2 * 4 * columns * 512 * other.shape[0]
    return call(early_kernel, [floats(4, columns, 512)], [], [other, scaled], flops=flops, name="early_products")[0]


def late_kernel(place, other, scaled, early, *rest):
    outs, total = rest[:4], rest[4]
    rows = early.shape[1]
    for t in range(4):
        total[:rows] = early[t]
        total[rows:] = product(other[...], scaled[t])
        scatter_blocks(place, total, outs, t)


def late_products(place, other, scaled, early):
    return call(
        late_kernel,
        block_shapes(4),
        [place],
        [other, scaled, early],
        [pltpu.VMEM((512, 512), jnp.float32)],
        flops=2 * 4 * 256 * 512 * other.shape[0],
        name="late_products",
    )


def far_products(place, other, scaled):
    return call(
        far_kernel,
        block_shapes(4),
        [place],
        [other, scaled],
        [pltpu.VMEM((512, 512), jnp.float32)],
        flops=2 * 4 * 512 * 512 * other.shape[0],
        name="far_products",
    )


def seal(outs, largest):
    divisor = jnp.clip(jnp.broadcast_to(largest, (16, T)) * 2.0**5, 2.0**-17, 2.0**15)
    divisor = divisor.astype(jnp.bfloat16).astype(jnp.float32)
    factor = (2.0**19 / divisor)[0:1]
    for out in outs:
        for row in range(0, out.shape[0] - 16, T):
            out[row : row + T] = out[row : row + T] * factor
        out[out.shape[0] - 16 :] = divisor


def sealed(count):
    return floats(count * T + 16, T)


def opened(value, start, count):
    end = start + count * T
    return value[start:end].astype(jnp.float32) * (value[end : end + 1].astype(jnp.float32) * 2.0**-19)


def halved(values):
    return [v.astype(jnp.float16) for v in values]


def largest_of(values):
    peak = functools.reduce(jnp.maximum, [jnp.abs(v) for v in values])
    return jnp.max(jnp.max(peak, axis=0, keepdims=True), axis=1, keepdims=True)


def first_sum_kernel(kept, a, b, c, *outs):
    peak = jnp.zeros((T, T), jnp.float32)
    for e in range(4):
        for n in range(kept.shape[1]):
            value = kept[e, n] + (a[e, n].astype(jnp.float32) + b[e, n].astype(jnp.float32)) + c[e, n].astype(jnp.float32)
            outs[e][n * T : (n + 1) * T] = value
            if e > 0:
                peak = jnp.maximum(peak, jnp.abs(value))
    seal(outs[1:], largest_of([peak]))


def first_sum(kept, a, b, c):
    count = kept.shape[1]
    kept, *send = call(
        first_sum_kernel,
        [floats(count * T, T)] + [sealed(count)] * 3,
        [],
        [kept, a, b, c],
        flops=20 * count * T * T,
        name="first_sum",
    )
    return kept, halved(send)


def seal_kernel(value, out):
    peak = jnp.zeros((T, T), jnp.float32)
    for row in range(0, value.shape[0], T):
        out[row : row + T] = value[row : row + T]
        peak = jnp.maximum(peak, jnp.abs(value[row : row + T]))
    seal([out], largest_of([peak]))


def across(value, at_home):
    pairs = [(s, d) for s, d in swap_perm(dy=1) if ((d >> 6) == (d & 3) >> 1) == at_home]
    count = value.shape[0] // T
    send = call(seal_kernel, [sealed(count)], [], [value], flops=2 * count * T * T, name="seal")
    return value + opened(permute(halved(send)[0], pairs), 0, count)


def pack_kernel(place, near, twin, far, *rest):
    outs, ready = rest[:4], rest[4]
    at_home = place[4] == 1
    block = lambda part, n: part[n * T : (n + 1) * T]

    @pl.when(at_home)
    def _():
        core = place[3]
        for f in range(FREQ):
            low, both, high = (block(near, 3 * f + j) for j in range(3))
            ready[0, f, 0] = low
            ready[0, f, 1] = both
            ready[1, f, 0] = both.T
            ready[1, f, 1] = high.T
        for k in range(2):
            for h in range(2):
                ready[2 + k, core, h] = block(near, 6 + 2 * h + k).T
                ready[2 + k, 1 - core, h] = block(twin, 2 * k + h)

    @pl.when(jnp.logical_not(at_home))
    def _():
        for half in range(2):
            for f in range(FREQ):
                for h in range(2):
                    value = block(far, 4 * half + 2 * f + h)
                    ready[half, f, h] = value
                    ready[2 + h, f, half] = value.T

    peak = jnp.zeros((T, T), jnp.float32)
    for k in range(4):
        for f in range(FREQ):
            for h in range(2):
                value = ready[place[5 + k], f, h]
                row = (2 * f + h) * T
                outs[k][row : row + T] = value
                peak = jnp.maximum(peak, jnp.abs(value))
    seal(outs, largest_of([peak]))


def pack(place, *arrays):
    return halved(
        call(
            pack_kernel,
            [sealed(2 * FREQ)] * 4,
            [place],
            arrays,
            [pltpu.VMEM((4, FREQ, 2, T, T), jnp.float32)],
            flops=2**20,
            name="pack",
        )
    )


def unpack_kernel(place, a, b, c, d, out):
    for k, arrived in enumerate((a, b, c, d)):
        for f in range(FREQ):
            for h in range(2):
                out[:, f, pl.ds(pl.multiple_of(512 * h + place[9 + k] * T, T), T)] = arrived[(2 * f + h) * T : (2 * f + h + 1) * T]


def unpack(place, arrived):
    arrived = [opened(v, 0, 2 * FREQ) for v in arrived]
    return call(unpack_kernel, [floats(T, FREQ, 1024)], [place], arrived, flops=2**18, name="unpack")[0]


def after(value, earlier):
    return value if earlier is None else lax.optimization_barrier((value, earlier))[0]


def send_first(send, earlier):
    return [permute(after(v, w), swap_perm(d1=d + 1)) for d, (v, w) in enumerate(zip(send, earlier))]


def send_second(send, earlier):
    return [permute(after(v, w), swap_perm(d2=e + 1)) for e, (v, w) in enumerate(zip(send, earlier))]


def on_device(own, energy_gaps, frequencies):
    blk, grp = lax.axis_index("blk"), lax.axis_index("grp")
    x, z, y_hi, core = blk & 3, (blk >> 2) & 3, blk >> 4, grp & 1
    perms, sent, filled = rounds()
    tables = lax.dynamic_index_in_dim(jnp.asarray(np.concatenate([sent, filled]).T), blk * 4 + grp, 0, keepdims=False)
    home = jnp.where(y_hi == grp >> 1, 1, 0)
    here = jnp.stack([jnp.where(core == 0, x, z), jnp.where(core == 0, z, x), y_hi, core, home]).astype(jnp.int32)
    place = jnp.concatenate([here, tables])

    swap, far_perm = group_perm(lambda g: g ^ 1), group_perm(lambda g: FAR[g])
    low = own[:, :512]
    own, low = lax.optimization_barrier((own, low))
    other = permute(own, swap)
    far0 = permute(low, far_perm)

    scaled, *blocks = own_products(here, frequencies, own, energy_gaps)
    near, *send = mate_products(place, other, scaled, blocks)
    rest = after(own, near)
    far1 = permute(after(rest[:, 512:768], far0), far_perm)
    near_sent = send_first(send, [None, None, None])
    sum0, *send = far_products(place, far0, scaled)
    far2 = permute(after(rest[:, 768:], sum0), far_perm)
    sum0_sent = send_first(send, near_sent)
    near, send = first_sum(near, *near_sent)
    near_sent = send_second(send, [sum0_sent[0], sum0_sent[1], sum0_sent[2]])
    sum0, send0 = first_sum(sum0, *sum0_sent)
    early = early_products(far1, scaled)
    sum1, *send = late_products(place, far2, scaled, early)
    sum1_sent = send_first(send, near_sent)
    sum1, send1 = first_sum(sum1, *sum1_sent)
    for v in near_sent:
        near = near + opened(v, 0, 10)
    near = across(after(near, sum1_sent[2]), True)
    twin = permute(near[6 * T :], swap)
    for v in send_second([jnp.concatenate(v) for v in zip(send0, send1)], [None]*3):
        sum0 = sum0 + opened(v, 0, 4)
        sum1 = sum1 + opened(v, 4 * T + 16, 4)
    far = across(jnp.concatenate([sum0, sum1]), False)
    packed = pack(place, near, twin, far)
    return unpack(place, [permute(v, p) for v, p in zip(packed, perms)])


def solution(mesh):
    in_specs = (P("blk", "grp"), P("blk"), P())
    out_specs = P("blk", None, "grp")
    return jax.shard_map(
        on_device, mesh=mesh, in_specs=in_specs, out_specs=out_specs, check_vma=False
    )
```

```python
import functools

import jax
import jax.numpy as jnp
import numpy as np
from jax import lax
from jax.experimental import pallas as pl
from jax.experimental.pallas import tpu as pltpu
from jax.sharding import PartitionSpec as P

AXES = ("blk", "grp")
FREQ = 2
T = 128
FAR = (2, 3, 1, 0)
VMEM = 8 * 1024 * 1024


def parts_of(d):
    x, z, y_hi, grp = (d >> 2) & 3, (d >> 4) & 3, d >> 6, d & 3
    return (y_hi, x, z, grp) if grp & 1 == 0 else (y_hi, z, x, grp)


def device(y_hi, s1, s2, grp):
    x, z = (s1, s2) if grp & 1 == 0 else (s2, s1)
    return (((y_hi * 4 + z) * 4 + x) << 2) + grp


def swap_perm(d1=0, d2=0, dy=0):
    pairs = []
    for d in range(128):
        y_hi, s1, s2, grp = parts_of(d)
        pairs.append((d, device(y_hi ^ dy, s1 ^ d1, s2 ^ d2, grp)))
    return pairs


def group_perm(source):
    return [(blk * 4 + source(grp), blk * 4 + grp) for blk in range(32) for grp in range(4)]


def block_of(core, s1, s2):
    skew = (s1 + s2) & 3
    return (s1, skew) if core == 0 else (skew, s2)


def messages(d):
    y_hi, s1, s2, g = parts_of(d)
    s1, s2 = block_of(g & 1, s1, s2)
    row = lambda group, half, block, grp: (8 * group + 4 * half + block) * 4 + grp
    if y_hi == g >> 1:
        return [
            (row(g, 0, s1, g), s2),
            (row(g, 1, s2, g), s1),
            (row(g, 0, s2, g ^ 1), s1),
            (row(g, 1, s2, g ^ 1), s1),
        ]
    far = FAR[g]
    return [
        (row(far, 0, s1, g), s2),
        (row(far, 1, s1, g), s2),
        (row(g, 0, s2, far), s1),
        (row(g, 1, s2, far), s1),
    ]


@functools.cache
def rounds():
    perms, sent, filled = [], np.zeros((4, 128), np.int32), np.zeros((4, 128), np.int32)
    for k in range(4):
        pairs = []
        for d in range(128):
            sent[k, d] = (0, 1, 3, 2)[((d >> 4) & 3) ^ k]
            to, slot = messages(d)[sent[k, d]]
            filled[k, to] = slot
            pairs.append((d, to))
        perms.append(pairs)
    return perms, sent, filled


def permute(value, pairs):
    return lax.ppermute(value, AXES, pairs)


def call(kernel, out_shape, scalars, arrays, scratch=(), flops=0, name=None, aliases=()):
    vmem, smem = pl.BlockSpec(memory_space=pltpu.VMEM), pl.BlockSpec(memory_space=pltpu.SMEM)
    size = 0
    return pl.pallas_call(
        kernel,
        out_shape=out_shape,
        in_specs=[smem] * len(scalars) + [vmem] * len(arrays),
        out_specs=[vmem] * len(out_shape),
        scratch_shapes=list(scratch),
        input_output_aliases=dict(aliases),
        compiler_params=pltpu.CompilerParams(vmem_limit_bytes=VMEM),
        cost_estimate=pl.CostEstimate(flops=flops, bytes_accessed=size, transcendentals=0),
        name=name,
    )(*scalars, *arrays)


def floats(*shape):
    return jax.ShapeDtypeStruct(shape, jnp.float32)


def product(lhs, rhs):
    return lax.dot_general(lhs, rhs, (((0,), (0,)), ((), ())), preferred_element_type=jnp.float32)


def scatter_blocks(place, total, outs, n):
    for d in range(4):
        for e in range(4):
            s1, s2 = place[0] ^ d, place[1] ^ e
            skew = (s1 + s2) & 3
            rows = pl.ds(pl.multiple_of(jnp.where(place[3] == 0, s1, skew) * T, T), T)
            columns = pl.ds(pl.multiple_of(jnp.where(place[3] == 0, skew, s2) * T, T), T)
            outs[d][e, n] = total[rows, columns].astype(outs[d].dtype)


def block_shapes(count):
    return [jax.ShapeDtypeStruct((4, count, T, T), jnp.float32 if d == 0 else jnp.bfloat16) for d in range(4)]


def own_kernel(place, frequencies, own, gaps, scaled, *rest):
    outs, total = rest[:4], rest[4]
    gap = jnp.broadcast_to(gaps[...], (8, gaps.shape[1]))
    weights = [(4.0 * gap / (gap * gap + frequencies[f] * frequencies[f])).T[:, 0:1] for f in range(FREQ)]
    for h in range(2):
        for f in range(FREQ):
            part = 2 * f + h
            scaled[part] = (own[:, 512 * h : 512 * (h + 1)].astype(jnp.float32) * weights[f]).astype(jnp.bfloat16)
            total[...] = product(own[:, :512], scaled[part])
            scatter_blocks(place, total, outs, f * 3 + h)
            if h == 1:
                total[...] = product(own[:, 512:], scaled[part])
                scatter_blocks(place, total, outs, f * 3 + 2)


def own_products(place, frequencies, own, gaps):
    rows = own.shape[0]
    return call(
        own_kernel,
        [jax.ShapeDtypeStruct((4, rows, 512), jnp.bfloat16)] + block_shapes(10),
        [place, frequencies],
        [own, gaps.reshape(1, rows)],
        [pltpu.VMEM((512, 512), jnp.float32)],
        flops=2 * 6 * 512 * 512 * rows,
        name="own_products",
    )


def mate_kernel(place, other, scaled, *rest):
    outs, total = rest[4:8], rest[8]

    for t in range(4):
        half = slice(t // 2 * 512, t // 2 * 512 + 512)
        total[...] = product(other[:, half], scaled[2 * place[3] + t % 2])
        scatter_blocks(place, total, outs, 6 + t)


def mate_products(place, other, scaled, blocks):
    return call(
        mate_kernel,
        block_shapes(10),
        [place],
        [other, scaled, *blocks],
        [pltpu.VMEM((512, 512), jnp.float32)],
        flops=2 * 4 * 512 * 512 * other.shape[0],
        name="mate_products",
        aliases={3 + d: d for d in range(4)},
    )


def far_kernel(place, other, scaled, *rest):
    outs, total = rest[:4], rest[4]

    def step(t, _):
        total[...] = product(other[...], scaled[t])
        scatter_blocks(place, total, outs, t)
        return 0

    lax.fori_loop(0, 4, step, 0)


def early_kernel(other, scaled, out):
    for t in range(4):
        out[t] = product(other[...], scaled[t])


def early_products(other, scaled):
    columns = other.shape[1]
    flops = 2 * 4 * columns * 512 * other.shape[0]
    return call(early_kernel, [floats(4, columns, 512)], [], [other, scaled], flops=flops, name="early_products")[0]


def late_kernel(place, other, scaled, early, *rest):
    outs, total = rest[:4], rest[4]
    rows = early.shape[1]
    for t in range(4):
        total[:rows] = early[t]
        total[rows:] = product(other[...], scaled[t])
        scatter_blocks(place, total, outs, t)


def late_products(place, other, scaled, early):
    return call(
        late_kernel,
        block_shapes(4),
        [place],
        [other, scaled, early],
        [pltpu.VMEM((512, 512), jnp.float32)],
        flops=2 * 4 * other.shape[1] * 512 * other.shape[0],
        name="late_products",
    )


def far_products(place, other, scaled):
    return call(
        far_kernel,
        block_shapes(4),
        [place],
        [other, scaled],
        [pltpu.VMEM((512, 512), jnp.float32)],
        flops=2 * 4 * 512 * 512 * other.shape[0],
        name="far_products",
    )


def seal(outs, largest):
    divisor = jnp.clip(jnp.broadcast_to(largest, (16, T)) * 2.0**5, 2.0**-17, 2.0**15)
    divisor = divisor.astype(jnp.bfloat16).astype(jnp.float32)
    factor = (2.0**19 / divisor)[0:1]
    for out in outs:
        for row in range(0, out.shape[0] - 16, T):
            out[row : row + T] = out[row : row + T] * factor
        out[out.shape[0] - 16 :] = divisor


def sealed(count):
    return floats(count * T + 16, T)


def opened(value, start, count):
    end = start + count * T
    return value[start:end].astype(jnp.float32) * (value[end : end + 1].astype(jnp.float32) * 2.0**-19)


def halved(values):
    return [v.astype(jnp.float16) for v in values]


def largest_of(values):
    peak = functools.reduce(jnp.maximum, [jnp.abs(v) for v in values])
    return jnp.max(jnp.max(peak, axis=0, keepdims=True), axis=1, keepdims=True)


def first_sum_kernel(kept, a, b, c, *outs):
    peak = jnp.zeros((T, T), jnp.float32)
    for e in range(4):
        for n in range(kept.shape[1]):
            value = kept[e, n] + (a[e, n].astype(jnp.float32) + b[e, n].astype(jnp.float32)) + c[e, n].astype(jnp.float32)
            outs[e][n * T : (n + 1) * T] = value
            if e > 0:
                peak = jnp.maximum(peak, jnp.abs(value))
    seal(outs[1:], largest_of([peak]))


def first_sum(kept, a, b, c):
    count = kept.shape[1]
    kept, *send = call(
        first_sum_kernel,
        [floats(count * T, T)] + [sealed(count)] * 3,
        [],
        [kept, a, b, c],
        flops=20 * count * T * T,
        name="first_sum",
    )
    return kept, halved(send)


def seal_kernel(value, out):
    peak = jnp.zeros((T, T), jnp.float32)
    for row in range(0, value.shape[0], T):
        out[row : row + T] = value[row : row + T]
        peak = jnp.maximum(peak, jnp.abs(value[row : row + T]))
    seal([out], largest_of([peak]))


def across(value, at_home):
    pairs = [(s, d) for s, d in swap_perm(dy=1) if ((d >> 6) == (d & 3) >> 1) == at_home]
    count = value.shape[0] // T
    send = call(seal_kernel, [sealed(count)], [], [value], flops=2 * count * T * T, name="seal")
    return value + opened(permute(halved(send)[0], pairs), 0, count)


def pack_kernel(place, near, twin, far, *rest):
    outs, ready = rest[:4], rest[4]
    at_home = place[4] == 1
    block = lambda part, n: part[n * T : (n + 1) * T]

    @pl.when(at_home)
    def _():
        core = place[3]
        for f in range(FREQ):
            low, both, high = (block(near, 3 * f + j) for j in range(3))
            ready[0, f, 0] = low
            ready[0, f, 1] = both
            ready[1, f, 0] = both.T
            ready[1, f, 1] = high.T
        for k in range(2):
            for h in range(2):
                ready[2 + k, core, h] = block(near, 6 + 2 * h + k).T
                ready[2 + k, 1 - core, h] = block(twin, 2 * k + h)

    @pl.when(jnp.logical_not(at_home))
    def _():
        for half in range(2):
            for f in range(FREQ):
                for h in range(2):
                    value = block(far, 4 * half + 2 * f + h)
                    ready[half, f, h] = value
                    ready[2 + h, f, half] = value.T

    peak = jnp.zeros((T, T), jnp.float32)
    for k in range(4):
        for f in range(FREQ):
            for h in range(2):
                value = ready[place[5 + k], f, h]
                row = (2 * f + h) * T
                outs[k][row : row + T] = value
                peak = jnp.maximum(peak, jnp.abs(value))
    seal(outs, largest_of([peak]))


def pack(place, *arrays):
    return halved(
        call(
            pack_kernel,
            [sealed(2 * FREQ)] * 4,
            [place],
            arrays,
            [pltpu.VMEM((4, FREQ, 2, T, T), jnp.float32)],
            flops=2**20,
            name="pack",
        )
    )


def unpack_kernel(place, a, b, c, d, out):
    for k, arrived in enumerate((a, b, c, d)):
        for f in range(FREQ):
            for h in range(2):
                out[:, f, pl.ds(pl.multiple_of(512 * h + place[9 + k] * T, T), T)] = arrived[(2 * f + h) * T : (2 * f + h + 1) * T]


def unpack(place, arrived):
    arrived = [opened(v, 0, 2 * FREQ) for v in arrived]
    return call(unpack_kernel, [floats(T, FREQ, 1024)], [place], arrived, flops=2**18, name="unpack")[0]


def after(value, earlier):
    return value if earlier is None else lax.optimization_barrier((value, earlier))[0]


def send_first(send, earlier):
    return [permute(after(v, w), swap_perm(d1=d + 1)) for d, (v, w) in enumerate(zip(send, earlier))]


def send_second(send, earlier):
    return [permute(after(v, w), swap_perm(d2=e + 1)) for e, (v, w) in enumerate(zip(send, earlier))]


def on_device(own, energy_gaps, frequencies):
    blk, grp = lax.axis_index("blk"), lax.axis_index("grp")
    x, z, y_hi, core = blk & 3, (blk >> 2) & 3, blk >> 4, grp & 1
    perms, sent, filled = rounds()
    tables = lax.dynamic_index_in_dim(jnp.asarray(np.concatenate([sent, filled]).T), blk * 4 + grp, 0, keepdims=False)
    home = jnp.where(y_hi == grp >> 1, 1, 0)
    here = jnp.stack([jnp.where(core == 0, x, z), jnp.where(core == 0, z, x), y_hi, core, home]).astype(jnp.int32)
    place = jnp.concatenate([here, tables])

    swap, far_perm = group_perm(lambda g: g ^ 1), group_perm(lambda g: FAR[g])
    low = own[:, :512]
    own, low = lax.optimization_barrier((own, low))
    other = permute(own, swap)
    far0 = permute(low, far_perm)

    scaled, *blocks = own_products(here, frequencies, own, energy_gaps)
    near, *send = mate_products(place, other, scaled, blocks)
    rest = after(own, near)
    far1 = permute(after(rest[:, 512:896], far0), far_perm)
    near_sent = send_first(send, [None, None, None])
    sum0, *send = far_products(place, far0, scaled)
    far2 = permute(after(rest[:, 896:], sum0), far_perm)
    sum0_sent = send_first(send, near_sent)
    near, send = first_sum(near, *near_sent)
    near_sent = send_second(send, [sum0_sent[0], sum0_sent[1], sum0_sent[2]])
    sum0, send0 = first_sum(sum0, *sum0_sent)
    early = early_products(far1, scaled)
    sum1, *send = late_products(place, far2, scaled, early)
    sum1_sent = send_first(send, near_sent)
    sum1, send1 = first_sum(sum1, *sum1_sent)
    for v in near_sent:
        near = near + opened(v, 0, 10)
    near = across(after(near, sum1_sent[2]), True)
    twin = permute(near[6 * T :], swap)
    for v in send_second([jnp.concatenate(v) for v in zip(send0, send1)], [None]*3):
        sum0 = sum0 + opened(v, 0, 4)
        sum1 = sum1 + opened(v, 4 * T + 16, 4)
    far = across(jnp.concatenate([sum0, sum1]), False)
    packed = pack(place, near, twin, far)
    return unpack(place, [permute(v, p) for v, p in zip(packed, perms)])


def solution(mesh):
    in_specs = (P("blk", "grp"), P("blk"), P())
    out_specs = P("blk", None, "grp")
    return jax.shard_map(
        on_device, mesh=mesh, in_specs=in_specs, out_specs=out_specs, check_vma=False
    )
```

```python
import functools

import jax
import jax.numpy as jnp
import numpy as np
from jax import lax
from jax.experimental import pallas as pl
from jax.experimental.pallas import tpu as pltpu
from jax.sharding import PartitionSpec as P

AXES = ("blk", "grp")
FREQ = 2
T = 128
FAR = (2, 3, 1, 0)
VMEM = 8 * 1024 * 1024


def parts_of(d):
    x, z, y_hi, grp = (d >> 2) & 3, (d >> 4) & 3, d >> 6, d & 3
    return (y_hi, x, z, grp) if grp & 1 == 0 else (y_hi, z, x, grp)


def device(y_hi, s1, s2, grp):
    x, z = (s1, s2) if grp & 1 == 0 else (s2, s1)
    return (((y_hi * 4 + z) * 4 + x) << 2) + grp


def swap_perm(d1=0, d2=0, dy=0):
    pairs = []
    for d in range(128):
        y_hi, s1, s2, grp = parts_of(d)
        pairs.append((d, device(y_hi ^ dy, s1 ^ d1, s2 ^ d2, grp)))
    return pairs


def group_perm(source):
    return [(blk * 4 + source(grp), blk * 4 + grp) for blk in range(32) for grp in range(4)]


def block_of(core, s1, s2):
    skew = (s1 + s2) & 3
    return (s1, skew) if core == 0 else (skew, s2)


def messages(d):
    y_hi, s1, s2, g = parts_of(d)
    s1, s2 = block_of(g & 1, s1, s2)
    row = lambda group, half, block, grp: (8 * group + 4 * half + block) * 4 + grp
    if y_hi == g >> 1:
        return [
            (row(g, 0, s1, g), s2),
            (row(g, 1, s2, g), s1),
            (row(g, 0, s2, g ^ 1), s1),
            (row(g, 1, s2, g ^ 1), s1),
        ]
    far = FAR[g]
    return [
        (row(far, 0, s1, g), s2),
        (row(far, 1, s1, g), s2),
        (row(g, 0, s2, far), s1),
        (row(g, 1, s2, far), s1),
    ]


@functools.cache
def rounds():
    perms, sent, filled = [], np.zeros((4, 128), np.int32), np.zeros((4, 128), np.int32)
    for k in range(4):
        pairs = []
        for d in range(128):
            sent[k, d] = (0, 1, 3, 2)[((d >> 4) & 3) ^ k]
            to, slot = messages(d)[sent[k, d]]
            filled[k, to] = slot
            pairs.append((d, to))
        perms.append(pairs)
    return perms, sent, filled


def permute(value, pairs):
    return lax.ppermute(value, AXES, pairs)


def call(kernel, out_shape, scalars, arrays, scratch=(), flops=0, name=None, aliases=()):
    vmem, smem = pl.BlockSpec(memory_space=pltpu.VMEM), pl.BlockSpec(memory_space=pltpu.SMEM)
    size = 0
    return pl.pallas_call(
        kernel,
        out_shape=out_shape,
        in_specs=[smem] * len(scalars) + [vmem] * len(arrays),
        out_specs=[vmem] * len(out_shape),
        scratch_shapes=list(scratch),
        input_output_aliases=dict(aliases),
        compiler_params=pltpu.CompilerParams(vmem_limit_bytes=VMEM),
        cost_estimate=pl.CostEstimate(flops=flops, bytes_accessed=size, transcendentals=0),
        name=name,
    )(*scalars, *arrays)


def floats(*shape):
    return jax.ShapeDtypeStruct(shape, jnp.float32)


def product(lhs, rhs):
    return lax.dot_general(lhs, rhs, (((0,), (0,)), ((), ())), preferred_element_type=jnp.float32)


def scatter_blocks(place, total, outs, n):
    for d in range(4):
        for e in range(4):
            s1, s2 = place[0] ^ d, place[1] ^ e
            skew = (s1 + s2) & 3
            rows = pl.ds(pl.multiple_of(jnp.where(place[3] == 0, s1, skew) * T, T), T)
            columns = pl.ds(pl.multiple_of(jnp.where(place[3] == 0, skew, s2) * T, T), T)
            outs[d][e, n] = total[rows, columns].astype(outs[d].dtype)


def block_shapes(count):
    return [jax.ShapeDtypeStruct((4, count, T, T), jnp.float32 if d == 0 else jnp.bfloat16) for d in range(4)]


def own_kernel(place, frequencies, own, gaps, scaled, *rest):
    outs, total = rest[:4], rest[4]
    gap = jnp.broadcast_to(gaps[...], (8, gaps.shape[1]))
    weights = [(4.0 * gap / (gap * gap + frequencies[f] * frequencies[f])).T[:, 0:1] for f in range(FREQ)]
    for h in range(2):
        for f in range(FREQ):
            part = 2 * f + h
            scaled[part] = (own[:, 512 * h : 512 * (h + 1)].astype(jnp.float32) * weights[f]).astype(jnp.bfloat16)
            total[...] = product(own[:, :512], scaled[part])
            scatter_blocks(place, total, outs, f * 3 + h)
            if h == 1:
                total[...] = product(own[:, 512:], scaled[part])
                scatter_blocks(place, total, outs, f * 3 + 2)


def own_products(place, frequencies, own, gaps):
    rows = own.shape[0]
    return call(
        own_kernel,
        [jax.ShapeDtypeStruct((4, rows, 512), jnp.bfloat16)] + block_shapes(10),
        [place, frequencies],
        [own, gaps.reshape(1, rows)],
        [pltpu.VMEM((512, 512), jnp.float32)],
        flops=2 * 6 * 512 * 512 * rows,
        name="own_products",
    )


def mate_kernel(place, other, scaled, *rest):
    outs, total = rest[4:8], rest[8]

    for t in range(4):
        half = slice(t // 2 * 512, t // 2 * 512 + 512)
        total[...] = product(other[:, half], scaled[2 * place[3] + t % 2])
        scatter_blocks(place, total, outs, 6 + t)


def mate_products(place, other, scaled, blocks):
    return call(
        mate_kernel,
        block_shapes(10),
        [place],
        [other, scaled, *blocks],
        [pltpu.VMEM((512, 512), jnp.float32)],
        flops=2 * 4 * 512 * 512 * other.shape[0],
        name="mate_products",
        aliases={3 + d: d for d in range(4)},
    )


def far_kernel(place, other, scaled, *rest):
    outs, total = rest[:4], rest[4]

    for t in range(4):
        total[...] = product(other[...], scaled[t])
        scatter_blocks(place, total, outs, t)


def early_kernel(other, scaled, out):
    for t in range(4):
        out[t] = product(other[...], scaled[t])


def early_products(other, scaled):
    columns = other.shape[1]
    flops = 2 * 4 * columns * 512 * other.shape[0]
    return call(early_kernel, [floats(4, columns, 512)], [], [other, scaled], flops=flops, name="early_products")[0]


def late_kernel(place, other, scaled, early, *rest):
    outs, total = rest[:4], rest[4]
    rows = early.shape[1]
    for t in range(4):
        total[:rows] = early[t]
        total[rows:] = product(other[...], scaled[t])
        scatter_blocks(place, total, outs, t)


def late_products(place, other, scaled, early):
    return call(
        late_kernel,
        block_shapes(4),
        [place],
        [other, scaled, early],
        [pltpu.VMEM((512, 512), jnp.float32)],
        flops=2 * 4 * other.shape[1] * 512 * other.shape[0],
        name="late_products",
    )


def far_products(place, other, scaled):
    return call(
        far_kernel,
        block_shapes(4),
        [place],
        [other, scaled],
        [pltpu.VMEM((512, 512), jnp.float32)],
        flops=2 * 4 * 512 * 512 * other.shape[0],
        name="far_products",
    )


def seal(outs, largest):
    divisor = jnp.clip(jnp.broadcast_to(largest, (16, T)) * 2.0**5, 2.0**-17, 2.0**15)
    divisor = divisor.astype(jnp.bfloat16).astype(jnp.float32)
    factor = (2.0**19 / divisor)[0:1]
    for out in outs:
        for row in range(0, out.shape[0] - 16, T):
            out[row : row + T] = out[row : row + T] * factor
        out[out.shape[0] - 16 :] = divisor


def sealed(count):
    return floats(count * T + 16, T)


def opened(value, start, count):
    end = start + count * T
    return value[start:end].astype(jnp.float32) * (value[end : end + 1].astype(jnp.float32) * 2.0**-19)


def halved(values):
    return [v.astype(jnp.float16) for v in values]


def largest_of(values):
    peak = functools.reduce(jnp.maximum, [jnp.abs(v) for v in values])
    return jnp.max(jnp.max(peak, axis=0, keepdims=True), axis=1, keepdims=True)


def first_sum_kernel(kept, a, b, c, *outs):
    peak = jnp.zeros((T, T), jnp.float32)
    for e in range(4):
        for n in range(kept.shape[1]):
            value = kept[e, n] + (a[e, n].astype(jnp.float32) + b[e, n].astype(jnp.float32)) + c[e, n].astype(jnp.float32)
            outs[e][n * T : (n + 1) * T] = value
            if e > 0:
                peak = jnp.maximum(peak, jnp.abs(value))
    seal(outs[1:], largest_of([peak]))


def first_sum(kept, a, b, c):
    count = kept.shape[1]
    kept, *send = call(
        first_sum_kernel,
        [floats(count * T, T)] + [sealed(count)] * 3,
        [],
        [kept, a, b, c],
        flops=20 * count * T * T,
        name="first_sum",
    )
    return kept, halved(send)


def seal_kernel(value, out):
    peak = jnp.zeros((T, T), jnp.float32)
    for row in range(0, value.shape[0], T):
        out[row : row + T] = value[row : row + T]
        peak = jnp.maximum(peak, jnp.abs(value[row : row + T]))
    seal([out], largest_of([peak]))


def across(value, at_home):
    pairs = [(s, d) for s, d in swap_perm(dy=1) if ((d >> 6) == (d & 3) >> 1) == at_home]
    count = value.shape[0] // T
    send = call(seal_kernel, [sealed(count)], [], [value], flops=2 * count * T * T, name="seal")
    return value + opened(permute(halved(send)[0], pairs), 0, count)


def pack_kernel(place, near, twin, far, *rest):
    outs, ready = rest[:4], rest[4]
    at_home = place[4] == 1
    block = lambda part, n: part[n * T : (n + 1) * T]

    @pl.when(at_home)
    def _():
        core = place[3]
        for f in range(FREQ):
            low, both, high = (block(near, 3 * f + j) for j in range(3))
            ready[0, f, 0] = low
            ready[0, f, 1] = both
            ready[1, f, 0] = both.T
            ready[1, f, 1] = high.T
        for k in range(2):
            for h in range(2):
                ready[2 + k, core, h] = block(near, 6 + 2 * h + k).T
                ready[2 + k, 1 - core, h] = block(twin, 2 * k + h)

    @pl.when(jnp.logical_not(at_home))
    def _():
        for half in range(2):
            for f in range(FREQ):
                for h in range(2):
                    value = block(far, 4 * half + 2 * f + h)
                    ready[half, f, h] = value
                    ready[2 + h, f, half] = value.T

    peak = jnp.zeros((T, T), jnp.float32)
    for k in range(4):
        for f in range(FREQ):
            for h in range(2):
                value = ready[place[5 + k], f, h]
                row = (2 * f + h) * T
                outs[k][row : row + T] = value
                peak = jnp.maximum(peak, jnp.abs(value))
    seal(outs, largest_of([peak]))


def pack(place, *arrays):
    return halved(
        call(
            pack_kernel,
            [sealed(2 * FREQ)] * 4,
            [place],
            arrays,
            [pltpu.VMEM((4, FREQ, 2, T, T), jnp.float32)],
            flops=2**20,
            name="pack",
        )
    )


def unpack_kernel(place, a, b, c, d, out):
    for k, arrived in enumerate((a, b, c, d)):
        for f in range(FREQ):
            for h in range(2):
                out[:, f, pl.ds(pl.multiple_of(512 * h + place[9 + k] * T, T), T)] = arrived[(2 * f + h) * T : (2 * f + h + 1) * T]


def unpack(place, arrived):
    arrived = [opened(v, 0, 2 * FREQ) for v in arrived]
    return call(unpack_kernel, [floats(T, FREQ, 1024)], [place], arrived, flops=2**18, name="unpack")[0]


def after(value, earlier):
    return value if earlier is None else lax.optimization_barrier((value, earlier))[0]


def send_first(send, earlier):
    return [permute(after(v, w), swap_perm(d1=d + 1)) for d, (v, w) in enumerate(zip(send, earlier))]


def send_second(send, earlier):
    return [permute(after(v, w), swap_perm(d2=e + 1)) for e, (v, w) in enumerate(zip(send, earlier))]


def on_device(own, energy_gaps, frequencies):
    blk, grp = lax.axis_index("blk"), lax.axis_index("grp")
    x, z, y_hi, core = blk & 3, (blk >> 2) & 3, blk >> 4, grp & 1
    perms, sent, filled = rounds()
    tables = lax.dynamic_index_in_dim(jnp.asarray(np.concatenate([sent, filled]).T), blk * 4 + grp, 0, keepdims=False)
    home = jnp.where(y_hi == grp >> 1, 1, 0)
    here = jnp.stack([jnp.where(core == 0, x, z), jnp.where(core == 0, z, x), y_hi, core, home]).astype(jnp.int32)
    place = jnp.concatenate([here, tables])

    swap, far_perm = group_perm(lambda g: g ^ 1), group_perm(lambda g: FAR[g])
    low = own[:, :512]
    own, low = lax.optimization_barrier((own, low))
    other = permute(own, swap)
    far0 = permute(low, far_perm)

    scaled, *blocks = own_products(here, frequencies, own, energy_gaps)
    near, *send = mate_products(place, other, scaled, blocks)
    rest = after(own, near)
    far1 = permute(after(rest[:, 512:896], far0), far_perm)
    near_sent = send_first(send, [None, None, None])
    sum0, *send = far_products(place, far0, scaled)
    far2 = permute(after(rest[:, 896:], sum0), far_perm)
    sum0_sent = send_first(send, near_sent)
    near, send = first_sum(near, *near_sent)
    near_sent = send_second(send, [sum0_sent[0], sum0_sent[1], sum0_sent[2]])
    sum0, send0 = first_sum(sum0, *sum0_sent)
    early = early_products(far1, scaled)
    sum1, *send = late_products(place, far2, scaled, early)
    sum1_sent = send_first(send, near_sent)
    sum1, send1 = first_sum(sum1, *sum1_sent)
    for v in near_sent:
        near = near + opened(v, 0, 10)
    near = across(after(near, sum1_sent[2]), True)
    twin = permute(near[6 * T :], swap)
    for v in send_second([jnp.concatenate(v) for v in zip(send0, send1)], [None]*3):
        sum0 = sum0 + opened(v, 0, 4)
        sum1 = sum1 + opened(v, 4 * T + 16, 4)
    far = across(jnp.concatenate([sum0, sum1]), False)
    packed = pack(place, near, twin, far)
    return unpack(place, [permute(v, p) for v, p in zip(packed, perms)])


def solution(mesh):
    in_specs = (P("blk", "grp"), P("blk"), P())
    out_specs = P("blk", None, "grp")
    return jax.shard_map(
        on_device, mesh=mesh, in_specs=in_specs, out_specs=out_specs, check_vma=False
    )
```
